128 devices in a mesh: pb: 16 (over z_hi, y, core), ka: 8 (over z_lo, x).
Axes of the slice: x: 4, y: 4, z: 4 (z_hi: 2, z_lo: 2; z = z_hi * 2 + z_lo), core: 2. Of those that a mesh axis runs over, the one named last changes fastest.
Arguments:
- queries: bfloat16 [16384, 4096], P('pb'), may hold values from -6 to 6
- key_rows: bfloat16 [16384, 512], P(('pb', 'ka')), may hold values from -6 to 6
- values: bfloat16 [16384, 512], P(('pb', 'ka')), may hold values from -6 to 6
- attn_out: bfloat16 [16384, 4096], P(('pb', 'ka')), may hold values from -6 to 6
- grad_out: bfloat16 [16384, 4096], P('pb'), may hold values from -6 to 6
- log_sums: float32 [32, 16384], P(None, ('pb', 'ka')), may hold values from 3 to 7
- key_gain: float32 [512], replicated, may hold values from 0.25 to 1.75
- value_gain: float32 [512], replicated, may hold values from 0.25 to 1.75
- doc_ids: int32 [128], replicated, may hold values from 0 to 15, never falling along the last dimension, each value on 1 to 64 neighbouring positions
- tile_mask: int32 [128, 128], replicated, may hold values 0 or 1
- block_order: int32 [128], replicated, may hold values from 0 to 127, each once
Outputs:
- grad_queries: bfloat16 [16384, 4096], P(('pb', 'ka'))
- grad_keys: bfloat16 [16384, 512], P(('pb', 'ka'))
- grad_values: bfloat16 [16384, 512], P(('pb', 'ka'))
- grad_key_gain: float32 [512], replicated
- grad_value_gain: float32 [512], replicated
The draws below stay inside these ranges and needn't reach their ends.
Inputs may be any that keep to these rules, and one draw needn't show every extreme that they name: `doc_ids`: documents are numbered in sequence order; each spans 1 to 64 tiles, one exactly that many. `block_order`: each sequence tile once.
All inputs are finite; a program needn't handle non-finite values.
Results may differ from the reference program's by a relative error of at most 0.015.
Values may be sent and summed in bfloat16 or wider, within the bound.
A program may use at most 192 MiB of HBM per device.

```python
import math
import jax
import jax.numpy as jnp
import numpy as np
from jax import lax

HEADS = 32
KV_HEADS = 4
HEAD_DIM = 128
TILE = 128
ROWS_DEV = 128
GROUP = 8
TOKENS = 16384
TILES = 128
N_KA = 8


def set_ends(values, key, smallest, largest):
    index_at = [jax.random.randint(jax.random.fold_in(key, axis), (), 0, length) for axis, length in enumerate(values.shape)]
    main_axis = values.shape.index(max(values.shape))
    neighbour = index_at[:main_axis] + [(index_at[main_axis] + 1) % values.shape[main_axis]] + index_at[main_axis + 1:]
    return values.at[tuple(index_at)].set(smallest).at[tuple(neighbour)].set(largest)


def block_scale(key, extent, split, low, high):
    gain, own = 1.0, jax.random.fold_in(key, 6)
    for axis_at, parts in split:
        heights = jnp.exp(jax.random.uniform(jax.random.fold_in(own, axis_at), (parts,), jnp.float32, low / len(split), high / len(split)))
        gain = gain * jnp.repeat(heights, extent[axis_at] // parts).reshape([-1 if axis == axis_at else 1 for axis in range(len(extent))])
    return gain


def split_up(number_of, total, limit, skew):
    loads = [(1 << 20) // math.isqrt(rank ** skew) + 1 for rank in range(2, number_of + 1)]
    surplus, holding = total - limit - (number_of - 1), [1] * (number_of - 1)
    while surplus > 0:
        movable = [i for i in range(number_of - 1) if holding[i] < limit]
        mass, remaining = sum([loads[i] for i in movable]), surplus
        for i in movable:
            addition = min(limit - holding[i], max(1, remaining * loads[i] // mass), surplus)
            holding[i] = holding[i] + addition
            surplus = surplus - addition
    return np.array([limit] + holding)


def ragged(stream_key, count, total, bound, slope):
    if count == 2:
        one = jax.random.randint(stream_key, (), max(1, total - bound), min(bound, total - 1) + 1)
        return jnp.stack([one, total - one])
    lengths = jnp.asarray(split_up(count, total, bound, slope), jnp.int32)
    pairs = (count - 1) // 2
    source_of, sink = lengths[1:1 + 2 * pairs:2], lengths[2:2 + 2 * pairs:2]
    slack = jnp.minimum(source_of - 1, bound - sink)
    passed = jax.random.randint(jax.random.fold_in(stream_key, 1), (pairs,), 0, 1 << 20) % (slack + 1)
    lengths = lengths.at[1:1 + 2 * pairs:2].set(source_of - passed).at[2:2 + 2 * pairs:2].set(sink + passed)
    return lengths[jax.random.permutation(jax.random.fold_in(stream_key, 2), count)]


def gaussian(own_key, dims, width, bound, shards=(), kind=jnp.bfloat16):
    factor_of = block_scale(own_key, dims, shards, -0.22, 0.18) if shards else 1.0
    values = jax.random.normal(own_key, dims, jnp.float32) * width * factor_of
    return jnp.minimum(jnp.maximum(values, -bound), bound).astype(kind)


def setup_inputs(seed: int = 0) -> dict:
    keys = jax.random.split(jax.random.key(seed), 12)
    queries = gaussian(keys[0], (TOKENS, HEADS * HEAD_DIM), 1.0, 6.0, ((0, 16),))
    key_rows = gaussian(keys[1], (TOKENS, KV_HEADS * HEAD_DIM), 1.0, 6.0, ((0, 128),))
    values = gaussian(keys[2], (TOKENS, KV_HEADS * HEAD_DIM), 1.0, 6.0, ((0, 128),))
    attn_out = gaussian(keys[3], (TOKENS, HEADS * HEAD_DIM), 1.0, 6.0, ((0, 128),))
    grad_out = gaussian(keys[4], (TOKENS, HEADS * HEAD_DIM), 1.0, 6.0, ((0, 16),))
    log_sums = jnp.clip(3.0 + 4.0 * jax.random.uniform(keys[5], (HEADS, TOKENS), jnp.float32) ** block_scale(keys[5], (HEADS, TOKENS), ((1, 128),), -0.2, 0.2), 3.0, 7.0)
    key_gain = jnp.clip(1.0 + 0.15 * jax.random.normal(keys[6], (KV_HEADS * HEAD_DIM,), jnp.float32), 0.25, 1.75)
    value_gain = jnp.clip(1.0 + 0.15 * jax.random.normal(keys[7], (KV_HEADS * HEAD_DIM,), jnp.float32), 0.25, 1.75)
    doc_ids = jnp.searchsorted(jnp.cumsum(ragged(keys[8], TILES // 8, TILES, TILES // 2, 2)), jnp.arange(TILES), side="right").astype(jnp.int32)
    tile_mask = set_ends((jax.random.randint(keys[9], (TILES, TILES), 0, 8) < 7).astype(jnp.int32), jax.random.fold_in(keys[9], 1), 0, 1)
    block_order = jax.random.permutation(keys[10], TILES).astype(jnp.int32)
    return dict(queries=queries, key_rows=key_rows, values=values, attn_out=attn_out, grad_out=grad_out, log_sums=log_sums, key_gain=key_gain, value_gain=value_gain, doc_ids=doc_ids, tile_mask=tile_mask, block_order=block_order)


def settle(value):
    return lax.optimization_barrier(value).astype(jnp.float32)


def add_rows(total, start, term):
    current = lax.dynamic_slice_in_dim(total, start, term.shape[0], 0)
    return lax.dynamic_update_slice_in_dim(total, current + term, start, 0)


def reference(queries, key_rows, values, attn_out, grad_out, log_sums, key_gain, value_gain, doc_ids, tile_mask, block_order):
    score_scale = HEAD_DIM ** -0.5
    feat_width = HEADS * HEAD_DIM
    kv_width = KV_HEADS * HEAD_DIM
    key_scaled = (key_rows.astype(jnp.float32) * key_gain).astype(jnp.bfloat16)
    value_scaled = (values.astype(jnp.float32) * value_gain).astype(jnp.bfloat16)
    products = grad_out.astype(jnp.float32) * attn_out.astype(jnp.float32)
    delta_rows = jnp.sum(products.reshape(TOKENS, HEADS, HEAD_DIM), axis=2).T
    tiles_block = ROWS_DEV // TILE
    offsets = jnp.arange(TILE, dtype=jnp.int32)
    loop_start = jnp.int32(0)
    loop_end = jnp.int32(TILES)

    def query_tile(query_at, totals):
        key_total, value_total, query_grads = totals
        seq_query = block_order[query_at]
        start_query = query_at * TILE
        query_tile_f = lax.dynamic_slice_in_dim(queries, start_query, TILE, 0).astype(jnp.float32).reshape(TILE, KV_HEADS, GROUP, HEAD_DIM)
        grad_tile = lax.dynamic_slice_in_dim(grad_out, start_query, TILE, 0).astype(jnp.float32).reshape(TILE, KV_HEADS, GROUP, HEAD_DIM)
        lse_tile = lax.dynamic_slice_in_dim(log_sums, start_query, TILE, 1).reshape(KV_HEADS, GROUP, TILE)
        delta_tile = lax.dynamic_slice_in_dim(delta_rows, start_query, TILE, 1).reshape(KV_HEADS, GROUP, TILE)
        query_pos = seq_query * TILE + offsets

        def key_tile(key_at, partial_value):
            seq_key = block_order[key_at]
            is_live = (tile_mask[seq_query, seq_key] == 1) & (doc_ids[seq_query] == doc_ids[seq_key]) & (seq_query >= seq_key)

            def accumulate(kept):
                key_parts, key_sum, value_sum = kept
                start_key = key_at * TILE
                key_tile_f = lax.dynamic_slice_in_dim(key_scaled, start_key, TILE, 0).astype(jnp.float32).reshape(TILE, KV_HEADS, HEAD_DIM)
                value_tile_f = lax.dynamic_slice_in_dim(value_scaled, start_key, TILE, 0).astype(jnp.float32).reshape(TILE, KV_HEADS, HEAD_DIM)
                key_pos = seq_key * TILE + offsets
                allowed = query_pos[:, None] >= key_pos[None, :]
                scores = jnp.einsum("ihgd,jhd->hgij", query_tile_f, key_tile_f) * score_scale
                weights = jnp.where(allowed, jnp.exp(scores - lse_tile[..., None]), 0.0)
                dweights = jnp.einsum("ihgd,jhd->hgij", grad_tile, value_tile_f)
                dscores = weights * (dweights - delta_tile[..., None])
                weights_low = settle(weights.astype(jnp.bfloat16))
                dscores_low = settle(dscores.astype(jnp.bfloat16))
                value_term = jnp.einsum("hgij,ihgd->jhd", weights_low, grad_tile).reshape(TILE, kv_width)
                key_term = (jnp.einsum("hgij,ihgd->jhd", dscores_low, query_tile_f) * score_scale).reshape(TILE, kv_width)
                query_term = (jnp.einsum("hgij,jhd->ihgd", dscores_low, key_tile_f) * score_scale).reshape(TILE, feat_width)
                key_set = (key_at // tiles_block) % N_KA
                key_parts = key_parts.at[key_set].add(query_term)
                key_sum = add_rows(key_sum, start_key, key_term)
                value_sum = add_rows(value_sum, start_key, value_term)
                return key_parts, key_sum, value_sum

            return lax.cond(is_live, accumulate, lambda kept: kept, partial_value)

        empty_parts = jnp.zeros((N_KA, TILE, feat_width), jnp.float32)
        key_parts, key_total, value_total = lax.fori_loop(loop_start, loop_end, key_tile, (empty_parts, key_total, value_total))
        rounded = jnp.sum(settle(key_parts.astype(jnp.bfloat16)), axis=0)
        query_grads = lax.dynamic_update_slice_in_dim(query_grads, rounded.astype(jnp.bfloat16), start_query, 0)
        return key_total, value_total, query_grads

    start_totals = (jnp.zeros((TOKENS, kv_width), jnp.float32), jnp.zeros((TOKENS, kv_width), jnp.float32), jnp.zeros((TOKENS, feat_width), jnp.bfloat16))
    key_total, value_total, grad_queries = lax.fori_loop(loop_start, loop_end, query_tile, start_totals)
    grad_keys = (key_total * key_gain).astype(jnp.bfloat16)
    grad_values = (value_total * value_gain).astype(jnp.bfloat16)
    grad_key_gain = jnp.sum(key_total * key_rows.astype(jnp.float32), axis=0)
    grad_value_gain = jnp.sum(value_total * values.astype(jnp.float32), axis=0)
    return grad_queries, grad_keys, grad_values, grad_key_gain, grad_value_gain
```

```python
import functools
import math

import jax
import jax.numpy as jnp
from jax import lax
from jax.experimental import pallas as pl
from jax.experimental.pallas import tpu as pltpu
from jax.sharding import PartitionSpec as P


D = 128
T = 128
RING = 4
KA = 8
HEADS = 4
WIDTH = HEADS * D
QUERY_TILES = 16
KEY_TILES = 64
LOG2E = math.log2(math.e)
MESH = pl.DeviceIdType.MESH
F32 = jnp.float32
BF16 = jnp.bfloat16
NT = (((1,), (1,)), ((), ()))
TN = (((0,), (0,)), ((), ()))


def wrap(at):
    return lax.rem(at + RING, RING)


def place():
    pb, ka = lax.axis_index("pb"), lax.axis_index("ka")
    z = lax.div(pb, 8) * 2 + lax.div(ka, 4)
    return z, lax.rem(lax.div(pb, 2), 4), lax.rem(ka, 4), lax.rem(pb, 2)


def ident(z, y, x, c):
    return (lax.div(z, 2) * 8 + y * 2 + c, lax.rem(z, 2) * 4 + x)


def group_peers(z, y, x, c):
    ka = lax.rem(z, 2) * 4 + x
    peers = []
    for flip in range(2):
        for step in range(KA):
            if flip or step:
                to = lax.rem(ka + step, KA)
                core = 1 - c if flip else c
                peers.append((flip, step, ident(lax.div(z, 2) * 2 + lax.div(to, 4), y, lax.rem(to, 4), core)))
    return peers


def greet(devices):
    barrier = pltpu.get_barrier_semaphore()
    for device in devices:
        pl.semaphore_signal(barrier, inc=1, device_id=device, device_id_type=MESH)
    pl.semaphore_wait(barrier, len(devices))


class Lane:
    def __init__(self, sends, recvs, base):
        self.sends, self.recvs, self.base, self.out = sends, recvs, base, []

    def send(self, source, target, number, device):
        copy = pltpu.make_async_remote_copy(
            src_ref=source,
            dst_ref=target,
            send_sem=self.sends.at[self.base + number],
            recv_sem=self.recvs.at[self.base + number],
            device_id=device,
            device_id_type=MESH,
        )
        copy.start()
        self.out.append(copy)

    def arrive(self, target, number, device):
        pltpu.make_async_remote_copy(
            src_ref=target,
            dst_ref=target,
            send_sem=self.sends.at[self.base + number],
            recv_sem=self.recvs.at[self.base + number],
            device_id=device,
            device_id_type=MESH,
        ).wait_recv()

    def drain(self):
        for copy in self.out:
            copy.wait_send()
        self.out = []


class Spread(Lane):
    def setup(self, item, plus, minus):
        self.item, self.plus, self.minus = item, plus, minus
        half = item(0).shape[0] // 2
        self.first, self.second = pl.ds(0, half), pl.ds(half, half)
        return self

    def start(self):
        self.send(self.item(0), self.item(0), 0, self.plus)
        self.send(self.item(0), self.item(0), 1, self.minus)

    def relay_up(self):
        block = self.item(-1)
        self.arrive(block, 0, self.minus)
        self.send(block.at[self.first], block.at[self.first], 2, self.plus)

    def relay_down(self):
        block = self.item(1)
        self.arrive(block, 1, self.plus)
        self.send(block.at[self.second], block.at[self.second], 3, self.minus)

    def finish(self):
        block = self.item(2)
        self.arrive(block.at[self.first], 2, self.minus)
        self.arrive(block.at[self.second], 3, self.plus)


class Fold(Lane):
    def setup(self, half_of, put, land, plus, minus):
        self.half_of, self.put, self.land, self.plus, self.minus = half_of, put, land, plus, minus
        return self

    def start(self):
        self.send(self.half_of(2, 0), self.land.at[0], 0, self.plus)
        self.send(self.half_of(2, 1), self.land.at[1], 1, self.minus)
        self.send(self.half_of(1, 1), self.land.at[3], 3, self.plus)
        self.send(self.half_of(-1, 0), self.land.at[4], 4, self.minus)

    def relay(self):
        self.arrive(self.land.at[0], 0, self.minus)
        add_into(self.half_of(1, 0), [self.land.at[0]])
        self.send(self.half_of(1, 0), self.land.at[2], 2, self.plus)
        self.arrive(self.land.at[1], 1, self.plus)
        add_into(self.half_of(-1, 1), [self.land.at[1]])
        self.send(self.half_of(-1, 1), self.land.at[5], 5, self.minus)

    def finish(self):
        self.arrive(self.land.at[3], 3, self.minus)
        self.arrive(self.land.at[4], 4, self.plus)
        self.arrive(self.land.at[2], 2, self.minus)
        add_into(self.half_of(0, 0), [self.land.at[2], self.land.at[4]])
        self.arrive(self.land.at[5], 5, self.plus)
        add_into(self.half_of(0, 1), [self.land.at[3], self.land.at[5]])


def add_into(total, terms):
    rows = 256

    @pl.loop(0, total.shape[0] // rows)
    def _(n):
        at = pl.ds(pl.multiple_of(n * rows, rows), rows)
        value = total[at, :].astype(F32)
        for term in terms:
            value = value + term[at, :].astype(F32)
        total[at, :] = value.astype(total.dtype)


def head_columns(z, x):
    return pl.ds(pl.multiple_of((lax.rem(z, 2) * 4 + x * 8) * D, WIDTH), WIDTH)


def pair_table(z, y, x, c, docs, mask, order):
    z_hi = lax.div(z, 2)
    row = lax.broadcasted_iota(jnp.int32, (T, T), 0)
    col = lax.broadcasted_iota(jnp.int32, (T, T), 1)
    doc_cols = jnp.broadcast_to(docs[...].astype(F32), (T, T))
    live = (mask[...] == 1) & (doc_cols.T == doc_cols) & (row >= col)
    live = jnp.where(live, 1.0, 0.0).astype(BF16)
    holds = jnp.where(row == jnp.broadcast_to(order[...], (T, T)), 1.0, 0.0).astype(BF16)
    by_key = jnp.dot(live, holds, preferred_element_type=F32).astype(BF16)
    stored = lax.dot_general(holds, by_key, TN, preferred_element_type=F32).astype(BF16)
    small_row = lax.broadcasted_iota(jnp.int32, (QUERY_TILES, T), 0)
    small_col = lax.broadcasted_iota(jnp.int32, (QUERY_TILES, T), 1)
    first = (z_hi * 4 + y) * QUERY_TILES
    pick = jnp.where(small_col == small_row + first, 1.0, 0.0).astype(BF16)
    mine = jnp.dot(pick, stored, preferred_element_type=F32).astype(BF16)
    slot_z, slot_y, slot_x = col // 16, col // 4 % 4, col % 4
    source = (slot_z // 2) * 64 + slot_y * 16 + c * 8 + slot_z % 2 * 4 + slot_x
    spread = jnp.where((row == source) & (col < KEY_TILES), 1.0, 0.0).astype(BF16)
    pairs = jnp.dot(mine, spread, preferred_element_type=F32)
    own = ((z_hi * 2 + small_row % 8 // 4) * 4 + y) * 4 + small_row % 4
    is_own = (small_col == own) & (small_row // 8 == c)
    diag = jnp.sum(jnp.where(is_own, pairs, 0.0), axis=1, keepdims=True)
    rest = jnp.where(is_own, 0.0, pairs)
    upto = jnp.where(row <= col, 1.0, 0.0).astype(BF16)
    rank = jnp.dot(rest.astype(BF16), upto, preferred_element_type=F32)
    count = jnp.sum(rest, axis=1, keepdims=True)
    numbers = lax.broadcasted_iota(jnp.int32, (8, T), 1).astype(F32).astype(BF16)
    lists = []
    for i in range(QUERY_TILES):
        at = jnp.where(rest[i : i + 1, :] > 0.5, rank[i : i + 1, :] - 1.0, -1.0)
        chosen = jnp.where(jnp.broadcast_to(at, (T, T)) == row.astype(F32), 1.0, 0.0).astype(BF16)
        lists.append(lax.dot_general(numbers, chosen, NT, preferred_element_type=F32)[:1])
    table = jnp.concatenate(lists, axis=0)
    table = jnp.where(small_col == KEY_TILES, count, table)
    table = jnp.where(small_col == KEY_TILES + 1, diag, table)
    table = table.astype(jnp.int32)
    return jnp.where(small_col == KEY_TILES + 2, jnp.where(small_row // 8 == c, own, 0), table)


def gather(
    queries, grad_out, keys, values, attn_out, log_sums, key_gain, value_gain, docs, mask, order,
    qg, gg, kg, vg, stats, table,
    own_grad, key_parts, value_parts, stat_parts, sends, recvs, local,
):
    z, y, x, c = place()
    ka = lax.rem(z, 2) * 4 + x
    columns = head_columns(z, x)
    own_rows = pl.ds(pl.multiple_of(ka * T, T), T)
    locals_ = [
        pltpu.make_async_copy(grad_out.at[own_rows], own_grad, local.at[0]),
        pltpu.make_async_copy(queries.at[:, columns], qg.at[c], local.at[1]),
        pltpu.make_async_copy(grad_out.at[:, columns], gg.at[c], local.at[2]),
    ]
    for copy in locals_:
        copy.start()
    for j in range(RING):
        lanes = pl.ds(j * D, D)
        key_parts[j] = (keys[:, lanes].astype(F32) * key_gain[:, lanes]).astype(BF16)
        value_parts[j] = (values[:, lanes].astype(F32) * value_gain[:, lanes]).astype(BF16)

    peers = group_peers(z, y, x, c)
    y_plus, y_minus = ident(z, wrap(y + 1), x, c), ident(z, wrap(y - 1), x, c)
    z_plus, z_minus = ident(wrap(z + 1), y, x, c), ident(wrap(z - 1), y, x, c)
    far = ident(wrap(z + 2 * lax.rem(z, 2) - 1), y, x, c)
    greet([peer for _, _, peer in peers] + [y_plus, y_minus, far])

    slot = pl.ds(pl.multiple_of(x * T, T), T)
    across = Lane(sends, recvs, 0)
    for step in range(1, RING):
        to = wrap(x + step)
        across.send(key_parts.at[to], kg.at[z, y, slot], step - 1, ident(z, y, to, c))
        across.send(value_parts.at[to], vg.at[z, y, slot], step + 2, ident(z, y, to, c))
    kept = [
        pltpu.make_async_copy(key_parts.at[x], kg.at[z, y, slot], local.at[3]),
        pltpu.make_async_copy(value_parts.at[x], vg.at[z, y, slot], local.at[4]),
    ]
    for copy in kept:
        copy.start()
    sibling = ident(z, y, x, 1 - c)
    pair = Lane(sends, recvs, 6)
    pair.send(queries.at[:, columns], qg.at[c], 0, sibling)
    pair.send(grad_out.at[:, columns], gg.at[c], 1, sibling)

    locals_[0].wait()
    for to in range(KA):
        first = to % 4 * 8 + to // 4 * 4
        stat_parts[to, 0:HEADS, :] = log_sums[first : first + HEADS, :]
        for h in range(HEADS):
            lanes = pl.ds((first + h) * D, D)
            product = own_grad[:, lanes].astype(F32) * attn_out[:, lanes].astype(F32)
            stat_parts[to, HEADS + h : HEADS + h + 1, :] = jnp.sum(product.T, axis=0, keepdims=True)
    share = Lane(sends, recvs, 8)
    for flip, step, peer in peers:
        share.send(stat_parts.at[lax.rem(ka + step, KA)], stats.at[c * KA + ka], flip * KA + step, peer)
    keep_stats = pltpu.make_async_copy(stat_parts.at[ka], stats.at[c * KA + ka], local.at[5])
    keep_stats.start()

    for copy in kept:
        copy.wait()
    for step in range(1, RING):
        origin = wrap(x - step)
        came = pl.ds(pl.multiple_of(origin * T, T), T)
        across.arrive(kg.at[z, y, came], step - 1, ident(z, y, origin, c))
        across.arrive(vg.at[z, y, came], step + 2, ident(z, y, origin, c))

    def block(ref, dz, dy):
        return ref.at[wrap(z + dz), wrap(y + dy)]

    base = 24
    key_first = Spread(sends, recvs, base).setup(lambda o: block(kg, o, 0), z_plus, z_minus)
    value_first = Spread(sends, recvs, base + 4).setup(lambda o: block(vg, 0, o), y_plus, y_minus)
    key_then, value_then = {}, {}
    for n, off in enumerate((0, -1, 1, 2)):
        key_then[off] = Spread(sends, recvs, base + 8 + 4 * n).setup(
            lambda o, off=off: block(kg, off, o), y_plus, y_minus
        )
        value_then[off] = Spread(sends, recvs, base + 24 + 4 * n).setup(
            lambda o, off=off: block(vg, o, off), z_plus, z_minus
        )
    key_first.start()
    value_first.start()
    key_then[0].start()
    value_then[0].start()

    table[...] = pair_table(z, y, x, c, docs, mask, order)

    key_first.relay_up()
    value_first.relay_up()
    key_then[-1].start()
    value_then[-1].start()
    key_first.relay_down()
    value_first.relay_down()
    key_then[1].start()
    value_then[1].start()
    for off in (0,):
        key_then[off].relay_up()
        value_then[off].relay_up()
        key_then[off].relay_down()
        value_then[off].relay_down()
    key_first.finish()
    value_first.finish()
    key_then[2].start()
    value_then[2].start()
    for off in (-1, 1, 2):
        key_then[off].relay_up()
        value_then[off].relay_up()
        key_then[off].relay_down()
        value_then[off].relay_down()
    for off in (0, -1, 1, 2):
        key_then[off].finish()
        value_then[off].finish()

    pair.arrive(qg.at[1 - c], 0, sibling)
    pair.arrive(gg.at[1 - c], 1, sibling)
    for flip, step, _ in peers:
        origin = lax.rem(ka + KA - step, KA)
        core = 1 - c if flip else c
        from_ = ident(lax.div(z, 2) * 2 + lax.div(origin, 4), y, lax.rem(origin, 4), core)
        share.arrive(stats.at[core * KA + origin], flip * KA + step, from_)
    keep_stats.wait()
    for copy in locals_[1:]:
        copy.wait()
    for lane in [across, pair, share, key_first, value_first, *key_then.values(), *value_then.values()]:
        lane.drain()


def attend(table, stats, q_ref, g_ref, k_ref, v_ref, dq_ref, dk_ref, dv_ref, plan, dk_acc, dv_acc, dq_acc, held):
    scale = D ** -0.5

    dk_acc[...] = jnp.zeros_like(dk_acc)
    dv_acc[...] = jnp.zeros_like(dv_acc)
    dq_acc[...] = jnp.zeros_like(dq_acc)

    def stack(ref, i):
        rows = pl.ds(pl.multiple_of(i * T, T), T)
        return jnp.concatenate([ref[rows, h * D : (h + 1) * D] for h in range(HEADS)], axis=0)

    def tiles(ref, a, b):
        parts = [ref[pl.ds(pl.multiple_of(at * T, T), T), :] for at in (a, b)]
        return jnp.concatenate(parts, axis=0)

    def unpack(step):
        word = plan[step]
        return word >> 16, (word >> 8) & 63, word & 63, (word >> 14) & 1, (word >> 6) & 1

    def front(step, slot, masked):
        i, a, b, use_a, use_b = unpack(step)
        s = lax.dot_general(tiles(k_ref, a, b), stack(q_ref, i), NT, preferred_element_type=F32)
        dp = lax.dot_general(tiles(v_ref, a, b), stack(g_ref, i), NT, preferred_element_type=F32)
        lse = jnp.concatenate([stats[i, h : h + 1, :] for h in range(HEADS)], axis=1) * LOG2E
        delta = jnp.concatenate([stats[i, HEADS + h : HEADS + h + 1, :] for h in range(HEADS)], axis=1)
        p = jnp.exp2(s * (scale * LOG2E) - lse)
        if masked:
            row = lax.broadcasted_iota(jnp.int32, (T, T), 0)
            col = lax.broadcasted_iota(jnp.int32, (T, T), 1)
            ok_a = row < use_a * T
            ok_b = row <= col - (1 - use_b) * T
            ok = jnp.concatenate(
                [jnp.concatenate([ok_a] * HEADS, axis=1), jnp.concatenate([ok_b] * HEADS, axis=1)], axis=0
            )
            p = jnp.where(ok, p, 0.0)
        held[slot, 0] = p.astype(BF16)
        held[slot, 1] = (p * (dp - delta)).astype(BF16)

    def back(step, slot):
        i, a, b, _, _ = unpack(step)
        p, ds = held[slot, 0], held[slot, 1]
        dv = jnp.dot(p, stack(g_ref, i), preferred_element_type=F32)
        dk = jnp.dot(ds, stack(q_ref, i), preferred_element_type=F32)
        dq_acc[i] += lax.dot_general(tiles(k_ref, a, b), ds, TN, preferred_element_type=F32)
        for n, at in enumerate((a, b)):
            rows = pl.ds(pl.multiple_of(at * T, T), T)
            dv_acc[rows, :] += dv[n * T : (n + 1) * T]
            dk_acc[rows, :] += dk[n * T : (n + 1) * T]

    def run(steps, masked):
        plan[steps] = 0
        front(0, 0, masked)
        twos = lax.div(steps, 2)

        @pl.loop(0, twos)
        def _(u):
            front(2 * u + 1, 1, masked)
            back(2 * u, 0)
            front(2 * u + 2, 0, masked)
            back(2 * u + 1, 1)

        @pl.when(steps > 2 * twos)
        def _():
            back(steps - 1, 0)

    def list_whole(i, n):
        halves = lax.div(table[i, KEY_TILES], 2)

        def put(r, n):
            plan[n] = (i << 16) | (table[i, 2 * r] << 8) | table[i, 2 * r + 1]
            return n + 1

        return lax.fori_loop(0, halves, put, n)

    run(lax.fori_loop(0, QUERY_TILES, list_whole, jnp.int32(0)), False)

    def list_masked(i, n):
        count, diag = table[i, KEY_TILES], table[i, KEY_TILES + 1]
        odd = lax.rem(count, 2)
        last = table[i, jnp.maximum(count - 1, 0)]

        @pl.when(odd + diag > 0)
        def _():
            plan[n] = (i << 16) | (odd << 14) | (last << 8) | (diag << 6) | table[i, KEY_TILES + 2]

        return n + jnp.minimum(odd + diag, 1)

    run(lax.fori_loop(0, QUERY_TILES, list_masked, jnp.int32(0)), True)

    @pl.loop(0, QUERY_TILES)
    def _(i):
        rows = pl.ds(pl.multiple_of(i * T, T), T)
        for h in range(HEADS):
            lanes = slice(h * D, (h + 1) * D)
            dq_ref[rows, lanes] = (dq_acc[i, :, lanes].T * scale).astype(BF16)

    @pl.loop(0, KEY_TILES)
    def _(n):
        at = pl.ds(pl.multiple_of(n * T, T), T)
        dk_ref[at, :] = (dk_acc[at, :] * scale).astype(BF16)
        swapped = (lax.rem(lax.div(n, 4), 4) * 4 + lax.div(n, 16)) * 4 + lax.rem(n, 4)
        dv_ref[pl.ds(pl.multiple_of(swapped * T, T), T), :] = dv_acc[at, :].astype(BF16)


def scatter(
    dq, dk_whole, dv_whole, keys, values, key_gain, value_gain,
    grad_queries, grad_keys, grad_values, gains,
    dk, dv, dq_own, local, dq_in, land_k1, land_v1, land_k2, land_v2, parts, near, sums, total, sends, recvs,
):
    z, y, x, c = place()
    ka = lax.rem(z, 2) * 4 + x
    z_hi, z_lo = lax.div(z, 2), lax.rem(z, 2)
    own_block = pl.ds(pl.multiple_of(c * KA * T, KA * T), KA * T)
    loads = [
        pltpu.make_async_copy(dk_whole, dk, local.at[0]),
        pltpu.make_async_copy(dv_whole, dv, local.at[1]),
        pltpu.make_async_copy(dq.at[own_block], dq_own, local.at[2]),
    ]
    for copy in loads:
        copy.start()
    peers = group_peers(z, y, x, c)
    y_plus, y_minus = ident(z, wrap(y + 1), x, c), ident(z, wrap(y - 1), x, c)
    z_plus, z_minus = ident(wrap(z + 1), y, x, c), ident(wrap(z - 1), y, x, c)
    far = ident(wrap(z + 2 * z_lo - 1), y, x, c)
    others = []
    for flip in range(2):
        for step in range(RING):
            if flip or step:
                hi = 1 - z_hi if flip else z_hi
                others.append((flip, step, ident(hi * 2 + z_lo, wrap(y + step), x, c)))
    greet([peer for _, _, peer in peers] + [other for _, _, other in others] + [far])

    sibling = ident(z, y, x, 1 - c)
    pair = Lane(sends, recvs, 0)
    for n in range(KA):
        rows = pl.ds(pl.multiple_of((1 - c) * KA * T + n * T, T), T)
        pair.send(dq.at[rows], dq_in.at[n], n, sibling)

    half = 2 * RING * T

    def key_half(off, n):
        return dk.at[pl.ds(pl.multiple_of(wrap(z + off) * 4 * RING * T + n * 2 * RING * T, half), half)]

    def value_half(off, n):
        return dv.at[pl.ds(pl.multiple_of(wrap(y + off) * 4 * RING * T + n * 2 * RING * T, half), half)]

    key_first = Fold(sends, recvs, 16).setup(key_half, None, land_k1, z_plus, z_minus)
    value_first = Fold(sends, recvs, 22).setup(value_half, None, land_v1, y_plus, y_minus)
    loads[0].wait()
    key_first.start()
    loads[1].wait()
    value_first.start()
    loads[2].wait()

    lane_q = Lane(sends, recvs, 8)
    columns = head_columns(z, x)
    for n in range(KA):
        to = lax.rem(ka + n, KA)
        own_rows = dq_own.at[pl.ds(pl.multiple_of(to * T, T), T)]
        if n == 0:
            for m in range(KA):
                pair.arrive(dq_in.at[m], m, sibling)
        for h in range(HEADS):
            lanes = pl.ds(h * D, D)
            value = own_rows[:, lanes].astype(F32) + dq_in[to, :, lanes].astype(F32)
            dq_in[to, :, lanes] = value.astype(BF16)
        if n:
            peer = ident(z_hi * 2 + lax.div(to, 4), y, lax.rem(to, 4), c)
            lane_q.send(dq_in.at[to], grad_queries.at[:, columns], n, peer)
    grad_queries[:, columns] = dq_in[ka]

    key_first.relay()
    value_first.relay()
    key_first.finish()
    value_first.finish()

    def key_quarter(off, n):
        start = wrap(z) * 4 * RING * T + wrap(y + off) * RING * T + n * 2 * T
        return dk.at[pl.ds(pl.multiple_of(start, 2 * T), 2 * T)]

    def value_quarter(off, n):
        start = wrap(y) * 4 * RING * T + wrap(z + off) * RING * T + n * 2 * T
        return dv.at[pl.ds(pl.multiple_of(start, 2 * T), 2 * T)]

    key_then = Fold(sends, recvs, 28).setup(key_quarter, None, land_k2, y_plus, y_minus)
    value_then = Fold(sends, recvs, 34).setup(value_quarter, None, land_v2, z_plus, z_minus)
    key_then.start()
    value_then.start()
    key_then.relay()
    value_then.relay()
    key_then.finish()
    value_then.finish()

    across = Lane(sends, recvs, 40)
    block_k = pl.multiple_of((z * 4 + y) * RING * T, RING * T)
    block_v = pl.multiple_of((y * 4 + z) * RING * T, RING * T)
    for step in range(1, RING):
        to = wrap(x + step)
        across.send(dk.at[pl.ds(block_k + to * T, T)], parts.at[0, x], step - 1, ident(z, y, to, c))
        across.send(dv.at[pl.ds(block_v + to * T, T)], parts.at[1, x], step + 2, ident(z, y, to, c))
    parts[0, x] = dk[pl.ds(block_k + x * T, T), :]
    parts[1, x] = dv[pl.ds(block_v + x * T, T), :]
    for step in range(1, RING):
        origin = wrap(x - step)
        across.arrive(parts.at[0, origin], step - 1, ident(z, y, origin, c))
        across.arrive(parts.at[1, origin], step + 2, ident(z, y, origin, c))
    for n in range(RING):
        lanes = pl.ds(n * D, D)
        dkey, dvalue = parts[0, n].astype(F32), parts[1, n].astype(F32)
        grad_keys[:, lanes] = (dkey * key_gain[:, lanes]).astype(BF16)
        grad_values[:, lanes] = (dvalue * value_gain[:, lanes]).astype(BF16)
        sums[n : n + 1, :] = jnp.sum(dkey * keys[:, lanes].astype(F32), axis=0, keepdims=True)
        sums[4 + n : 5 + n, :] = jnp.sum(dvalue * values[:, lanes].astype(F32), axis=0, keepdims=True)

    mine = c * KA + ka
    share = Lane(sends, recvs, 46)
    for flip, step, peer in peers:
        share.send(sums, near.at[mine], flip * KA + step, peer)
    near[mine] = sums[...]
    for flip, step, _ in peers:
        origin = lax.rem(ka + KA - step, KA)
        core = 1 - c if flip else c
        from_ = ident(z_hi * 2 + lax.div(origin, 4), y, lax.rem(origin, 4), core)
        share.arrive(near.at[core * KA + origin], flip * KA + step, from_)
    total[0] = jnp.sum(near[...], axis=0)
    spread = Lane(sends, recvs, 62)
    mine = z_hi * RING + y
    for flip, step, other in others:
        spread.send(total.at[0], total.at[1 + mine], flip * RING + step, other)
    total[1 + mine] = total[0]
    for flip, step, _ in others:
        hi = 1 - z_hi if flip else z_hi
        origin = wrap(y - step)
        spread.arrive(total.at[1 + hi * RING + origin], flip * RING + step, ident(hi * 2 + z_lo, origin, x, c))
    gains[...] = jnp.sum(total[1:], axis=0)

    for n in range(1, KA):
        origin = lax.rem(ka + KA - n, KA)
        their = head_columns(lax.div(origin, 4), lax.rem(origin, 4))
        from_ = ident(z_hi * 2 + lax.div(origin, 4), y, lax.rem(origin, 4), c)
        lane_q.arrive(grad_queries.at[:, their], n, from_)
    for lane in [pair, lane_q, key_first, value_first, key_then, value_then, across, share, spread]:
        lane.drain()


def shape(dims, dtype):
    return jax.ShapeDtypeStruct(dims, dtype)


def shards(
    queries, key_rows, values, attn_out, grad_out, log_sums, key_gain, value_gain, doc_ids, tile_mask, block_order
):
    vm, hbm = pl.BlockSpec(memory_space=pltpu.VMEM), pl.BlockSpec(memory_space=pl.ANY)
    key_gain, value_gain = key_gain.reshape(1, -1), value_gain.reshape(1, -1)
    rows = queries.shape[0]
    qg, gg, kg, vg, stats, table = pl.pallas_call(
        gather,
        out_shape=(
            shape((2, rows, WIDTH), BF16),
            shape((2, rows, WIDTH), BF16),
            shape((RING, RING, RING * T, D), BF16),
            shape((RING, RING, RING * T, D), BF16),
            shape((QUERY_TILES, 2 * HEADS, T), F32),
            shape((QUERY_TILES, T), jnp.int32),
        ),
        in_specs=[hbm, hbm] + [vm] * 9,
        out_specs=(hbm, hbm, hbm, hbm, hbm, vm),
        scratch_shapes=[
            pltpu.VMEM(attn_out.shape, BF16),
            pltpu.VMEM((RING, T, D), BF16),
            pltpu.VMEM((RING, T, D), BF16),
            pltpu.VMEM((KA, 2 * HEADS, T), F32),
            pltpu.SemaphoreType.DMA((64,)),
            pltpu.SemaphoreType.DMA((64,)),
            pltpu.SemaphoreType.DMA((6,)),
        ],
        compiler_params=pltpu.CompilerParams(
            collective_id=0, has_side_effects=True, vmem_limit_bytes=32 * 2**20
        ),
        name="gather",
    )(
        queries, grad_out, key_rows, values, attn_out, log_sums, key_gain, value_gain,
        doc_ids.reshape(1, -1), tile_mask, block_order.reshape(1, -1),
    )
    dq, dk, dv = pl.pallas_call(
        attend,
        out_shape=(
            shape((2 * rows, WIDTH), BF16),
            shape((KEY_TILES * T, D), BF16),
            shape((KEY_TILES * T, D), BF16),
        ),
        in_specs=[pl.BlockSpec(memory_space=pltpu.SMEM)] + [vm] * 5,
        out_specs=(vm, vm, vm),
        scratch_shapes=[
            pltpu.SMEM((QUERY_TILES * KEY_TILES // 2 + 2,), jnp.int32),
            pltpu.VMEM((KEY_TILES * T, D), F32),
            pltpu.VMEM((KEY_TILES * T, D), F32),
            pltpu.VMEM((QUERY_TILES, D, WIDTH), F32),
            pltpu.VMEM((2, 2, 2 * T, WIDTH), BF16),
        ],
        compiler_params=pltpu.CompilerParams(vmem_limit_bytes=56 * 2**20),
        name="attend",
    )(
        table, stats, qg.reshape(2 * rows, WIDTH), gg.reshape(2 * rows, WIDTH),
        kg.reshape(KEY_TILES * T, D), vg.reshape(KEY_TILES * T, D),
    )
    grad_queries, grad_keys, grad_values, gains = pl.pallas_call(
        scatter,
        out_shape=(
            shape(attn_out.shape, BF16),
            shape(key_rows.shape, BF16),
            shape(values.shape, BF16),
            shape((2 * RING, D), F32),
        ),
        in_specs=[hbm] * 3 + [vm] * 4,
        out_specs=(vm, vm, vm, vm),
        scratch_shapes=[
            pltpu.VMEM((KEY_TILES * T, D), BF16),
            pltpu.VMEM((KEY_TILES * T, D), BF16),
            pltpu.VMEM((rows, WIDTH), BF16),
            pltpu.SemaphoreType.DMA((3,)),
            pltpu.VMEM((KA, T, WIDTH), BF16),
            pltpu.VMEM((6, 2 * RING * T, D), BF16),
            pltpu.VMEM((6, 2 * RING * T, D), BF16),
            pltpu.VMEM((6, 2 * T, D), BF16),
            pltpu.VMEM((6, 2 * T, D), BF16),
            pltpu.VMEM((2, RING, T, D), BF16),
            pltpu.VMEM((QUERY_TILES, 2 * RING, D), F32),
            pltpu.VMEM((2 * RING, D), F32),
            pltpu.VMEM((9, 2 * RING, D), F32),
            pltpu.SemaphoreType.DMA((70,)),
            pltpu.SemaphoreType.DMA((70,)),
        ],
        compiler_params=pltpu.CompilerParams(
            collective_id=1, has_side_effects=True, vmem_limit_bytes=48 * 2**20
        ),
        name="scatter",
    )(dq, dk, dv, key_rows, values, key_gain, value_gain)
    return grad_queries, grad_keys, grad_values, gains[:RING].reshape(-1), gains[RING:].reshape(-1)


def solution(mesh):
    rows = P(("pb", "ka"), None)
    placed = (P("pb", None), rows, rows, rows, P("pb", None), P(None, ("pb", "ka")), P(), P(), P(), P(), P())
    return jax.shard_map(
        shards, mesh=mesh, in_specs=placed, out_specs=(rows, rows, rows, P(), P()), check_vma=False
    )
```

```python
import functools
import math

import jax
import jax.numpy as jnp
from jax import lax
from jax.experimental import pallas as pl
from jax.experimental.pallas import tpu as pltpu
from jax.sharding import PartitionSpec as P


D = 128
T = 128
RING = 4
KA = 8
HEADS = 4
WIDTH = HEADS * D
QUERY_TILES = 16
KEY_TILES = 64
LOG2E = math.log2(math.e)
MESH = pl.DeviceIdType.MESH
F32 = jnp.float32
BF16 = jnp.bfloat16
NT = (((1,), (1,)), ((), ()))
TN = (((0,), (0,)), ((), ()))


def wrap(at):
    return lax.rem(at + RING, RING)


def place():
    pb, ka = lax.axis_index("pb"), lax.axis_index("ka")
    z = lax.div(pb, 8) * 2 + lax.div(ka, 4)
    return z, lax.rem(lax.div(pb, 2), 4), lax.rem(ka, 4), lax.rem(pb, 2)


def ident(z, y, x, c):
    return (lax.div(z, 2) * 8 + y * 2 + c, lax.rem(z, 2) * 4 + x)


def group_peers(z, y, x, c):
    ka = lax.rem(z, 2) * 4 + x
    peers = []
    for flip in range(2):
        for step in range(KA):
            if flip or step:
                to = lax.rem(ka + step, KA)
                core = 1 - c if flip else c
                peers.append((flip, step, ident(lax.div(z, 2) * 2 + lax.div(to, 4), y, lax.rem(to, 4), core)))
    return peers


def greet(devices):
    barrier = pltpu.get_barrier_semaphore()
    for device in devices:
        pl.semaphore_signal(barrier, inc=1, device_id=device, device_id_type=MESH)
    pl.semaphore_wait(barrier, len(devices))


class Lane:
    def __init__(self, sends, recvs, base):
        self.sends, self.recvs, self.base, self.out = sends, recvs, base, []

    def send(self, source, target, number, device):
        copy = pltpu.make_async_remote_copy(
            src_ref=source,
            dst_ref=target,
            send_sem=self.sends.at[self.base + number],
            recv_sem=self.recvs.at[self.base + number],
            device_id=device,
            device_id_type=MESH,
        )
        copy.start()
        self.out.append(copy)

    def arrive(self, target, number, device):
        pltpu.make_async_remote_copy(
            src_ref=target,
            dst_ref=target,
            send_sem=self.sends.at[self.base + number],
            recv_sem=self.recvs.at[self.base + number],
            device_id=device,
            device_id_type=MESH,
        ).wait_recv()

    def drain(self):
        for copy in self.out:
            copy.wait_send()
        self.out = []


class Spread(Lane):
    def setup(self, item, plus, minus):
        self.item, self.plus, self.minus = item, plus, minus
        half = item(0).shape[0] // 2
        self.first, self.second = pl.ds(0, half), pl.ds(half, half)
        return self

    def start(self):
        self.send(self.item(0), self.item(0), 0, self.plus)
        self.send(self.item(0), self.item(0), 1, self.minus)

    def relay_up(self):
        block = self.item(-1)
        self.arrive(block, 0, self.minus)
        self.send(block.at[self.first], block.at[self.first], 2, self.plus)

    def relay_down(self):
        block = self.item(1)
        self.arrive(block, 1, self.plus)
        self.send(block.at[self.second], block.at[self.second], 3, self.minus)

    def finish(self):
        block = self.item(2)
        self.arrive(block.at[self.first], 2, self.minus)
        self.arrive(block.at[self.second], 3, self.plus)


class Fold(Lane):
    def setup(self, half_of, land, plus, minus):
        self.half_of, self.land, self.plus, self.minus = half_of, land, plus, minus
        return self

    def start(self):
        self.send(self.half_of(2, 0), self.land.at[0], 0, self.plus)
        self.send(self.half_of(2, 1), self.land.at[1], 1, self.minus)
        self.send(self.half_of(1, 1), self.land.at[3], 3, self.plus)
        self.send(self.half_of(-1, 0), self.land.at[4], 4, self.minus)

    def relay(self):
        self.arrive(self.land.at[0], 0, self.minus)
        combine(self.land.at[0], [self.land.at[0], self.half_of(1, 0)])
        self.send(self.land.at[0], self.land.at[2], 2, self.plus)
        self.arrive(self.land.at[1], 1, self.plus)
        combine(self.land.at[1], [self.land.at[1], self.half_of(-1, 1)])
        self.send(self.land.at[1], self.land.at[5], 5, self.minus)

    def finish(self, factor=None):
        self.arrive(self.land.at[3], 3, self.minus)
        self.arrive(self.land.at[4], 4, self.plus)
        self.arrive(self.land.at[2], 2, self.minus)
        combine(self.land.at[2], [self.half_of(0, 0), self.land.at[2], self.land.at[4]], factor)
        self.arrive(self.land.at[5], 5, self.plus)
        combine(self.land.at[3], [self.half_of(0, 1), self.land.at[3], self.land.at[5]], factor)


class Detour(Lane):
    def setup(self, item, cuts, land, z, hi, lo):
        self.item, self.cuts, self.land, self.z, self.hi, self.lo = item, cuts, land, z, hi, lo
        side = 2 * lax.rem(z, 2) - 1
        self.at_hi, self.at_lo, self.at_far = wrap(z + side), wrap(z - side), wrap(z + 2)
        return self

    def start(self):
        for n, cut in enumerate(self.cuts):
            self.send(self.item(self.at_far).at[cut], self.land.at[0].at[cut], n, self.hi)
        self.send(self.item(self.at_hi), self.land.at[1], len(self.cuts), self.hi)

    def relay(self, n):
        cut = self.cuts[n]
        passed = self.land.at[0].at[cut]
        self.arrive(passed, n, self.hi)
        combine(passed, [passed, self.item(self.at_lo).at[cut]])
        self.send(passed, self.land.at[2].at[cut], len(self.cuts) + 1 + n, self.lo)

    def finish(self, total, factor=None):
        self.arrive(self.land.at[1], len(self.cuts), self.hi)
        for n, cut in enumerate(self.cuts):
            self.arrive(self.land.at[2].at[cut], len(self.cuts) + 1 + n, self.lo)
        combine(total, [self.item(self.z), self.land.at[1], self.land.at[2]], factor)


def combine(total, terms, factor=None):
    lead = total.shape[:-2]

    @pl.loop(0, math.prod(lead))
    def _(n):
        at = []
        for extent in reversed(lead):
            at.append(lax.rem(n, extent))
            n = lax.div(n, extent)
        at = tuple(reversed(at))
        value = terms[0][at].astype(F32)
        for term in terms[1:]:
            value = value + term[at].astype(F32)
        if factor is not None:
            value = value * factor
        total[at] = value.astype(total.dtype)


def head_columns(z, x):
    return pl.ds(pl.multiple_of((lax.rem(z, 2) * 4 + x * 8) * D, WIDTH), WIDTH)


def pair_table(z, y, x, c, docs, mask, order):
    z_hi = lax.div(z, 2)
    row = lax.broadcasted_iota(jnp.int32, (T, T), 0)
    col = lax.broadcasted_iota(jnp.int32, (T, T), 1)
    doc_cols = jnp.broadcast_to(docs[...].astype(F32), (T, T))
    live = (mask[...] == 1) & (doc_cols.T == doc_cols) & (row >= col)
    live = jnp.where(live, 1.0, 0.0).astype(BF16)
    holds = jnp.where(row == jnp.broadcast_to(order[...], (T, T)), 1.0, 0.0).astype(BF16)
    by_key = jnp.dot(live, holds, preferred_element_type=F32).astype(BF16)
    stored = lax.dot_general(holds, by_key, TN, preferred_element_type=F32).astype(BF16)
    small_row = lax.broadcasted_iota(jnp.int32, (QUERY_TILES, T), 0)
    small_col = lax.broadcasted_iota(jnp.int32, (QUERY_TILES, T), 1)
    first = (z_hi * 4 + y) * QUERY_TILES
    pick = jnp.where(small_col == small_row + first, 1.0, 0.0).astype(BF16)
    mine = jnp.dot(pick, stored, preferred_element_type=F32).astype(BF16)
    slot_z, slot_y, slot_x = col // 16, col // 4 % 4, col % 4
    source = (slot_z // 2) * 64 + slot_y * 16 + c * 8 + slot_z % 2 * 4 + slot_x
    spread = jnp.where((row == source) & (col < KEY_TILES), 1.0, 0.0).astype(BF16)
    pairs = jnp.dot(mine, spread, preferred_element_type=F32)
    own = ((z_hi * 2 + small_row % 8 // 4) * 4 + y) * 4 + small_row % 4
    is_own = (small_col == own) & (small_row // 8 == c)
    diag = jnp.sum(jnp.where(is_own, pairs, 0.0), axis=1, keepdims=True)
    rest = jnp.where(is_own, 0.0, pairs)
    upto = jnp.where(row <= col, 1.0, 0.0).astype(BF16)
    rank = jnp.dot(rest.astype(BF16), upto, preferred_element_type=F32)
    count = jnp.sum(rest, axis=1, keepdims=True)
    numbers = lax.broadcasted_iota(jnp.int32, (8, T), 1).astype(F32).astype(BF16)
    lists = []
    for i in range(QUERY_TILES):
        at = jnp.where(rest[i : i + 1, :] > 0.5, rank[i : i + 1, :] - 1.0, -1.0)
        chosen = jnp.where(jnp.broadcast_to(at, (T, T)) == row.astype(F32), 1.0, 0.0).astype(BF16)
        lists.append(lax.dot_general(numbers, chosen, NT, preferred_element_type=F32)[:1])
    table = jnp.concatenate(lists, axis=0)
    table = jnp.where(small_col == KEY_TILES, count, table)
    table = jnp.where(small_col == KEY_TILES + 1, diag, table)
    table = table.astype(jnp.int32)
    return jnp.where(small_col == KEY_TILES + 2, jnp.where(small_row // 8 == c, own, 0), table)


def gather(
    queries, grad_out, keys, values, attn_in, logs_in, docs_in, mask_in, order_in,
    sibling_rows, kg, vg, stats, table_out,
    table, attn_out, log_sums, docs, mask, order,
    own_grad, stat_parts, sends, recvs, local,
):
    z, y, x, c = place()
    ka = lax.rem(z, 2) * 4 + x
    columns = head_columns(z, x)
    own_rows = pl.ds(pl.multiple_of(ka * T, T), T)
    loads = [
        pltpu.make_async_copy(source, target, local.at[6 + n])
        for n, (source, target) in enumerate(
            (
                (attn_in, attn_out),
                (logs_in, log_sums),
                (docs_in, docs),
                (mask_in, mask),
                (order_in, order),
            )
        )
    ]
    loads.append(pltpu.make_async_copy(grad_out.at[own_rows], own_grad, local.at[0]))
    for copy in loads:
        copy.start()

    def part(ref, to):
        return ref.at[:, pl.ds(pl.multiple_of(to * D, D), D)]

    peers = group_peers(z, y, x, c)
    y_plus, y_minus = ident(z, wrap(y + 1), x, c), ident(z, wrap(y - 1), x, c)
    z_plus, z_minus = ident(wrap(z + 1), y, x, c), ident(wrap(z - 1), y, x, c)
    far = ident(wrap(z + 2 * lax.rem(z, 2) - 1), y, x, c)
    greet([peer for _, _, peer in peers] + [y_plus, y_minus, far])

    slot = pl.ds(pl.multiple_of(x * T, T), T)
    across = Lane(sends, recvs, 0)
    for step in range(1, RING):
        to = wrap(x + step)
        across.send(part(keys, to), kg.at[z, y, slot], step - 1, ident(z, y, to, c))
        across.send(part(values, to), vg.at[z, y, slot], step + 2, ident(z, y, to, c))
    kept = [
        pltpu.make_async_copy(part(keys, x), kg.at[z, y, slot], local.at[3]),
        pltpu.make_async_copy(part(values, x), vg.at[z, y, slot], local.at[4]),
    ]
    for copy in kept:
        copy.start()
    sibling = ident(z, y, x, 1 - c)
    pair = Lane(sends, recvs, 6)
    pair.send(queries.at[:, columns], sibling_rows.at[0], 0, sibling)
    pair.send(grad_out.at[:, columns], sibling_rows.at[1], 1, sibling)

    for copy in kept:
        copy.wait()
    for step in range(1, RING):
        origin = wrap(x - step)
        came = pl.ds(pl.multiple_of(origin * T, T), T)
        across.arrive(kg.at[z, y, came], step - 1, ident(z, y, origin, c))
        across.arrive(vg.at[z, y, came], step + 2, ident(z, y, origin, c))

    def block(ref, dz, dy):
        return ref.at[wrap(z + dz), wrap(y + dy)]

    base = 24
    key_first = Spread(sends, recvs, base).setup(lambda o: block(kg, o, 0), z_plus, z_minus)
    value_first = Spread(sends, recvs, base + 4).setup(lambda o: block(vg, 0, o), y_plus, y_minus)
    key_then, value_then = {}, {}
    for n, off in enumerate((0, -1, 1, 2)):
        key_then[off] = Spread(sends, recvs, base + 8 + 4 * n).setup(
            lambda o, off=off: block(kg, off, o), y_plus, y_minus
        )
        value_then[off] = Spread(sends, recvs, base + 24 + 4 * n).setup(
            lambda o, off=off: block(vg, o, off), z_plus, z_minus
        )
    key_first.start()
    value_first.start()
    key_then[0].start()
    value_then[0].start()

    for copy in loads:
        copy.wait()
    for to in range(KA):
        first = to % 4 * 8 + to // 4 * 4
        stat_parts[to, 0:HEADS, :] = log_sums[first : first + HEADS, :]
        for h in range(HEADS):
            lanes = pl.ds((first + h) * D, D)
            product = own_grad[:, lanes].astype(F32) * attn_out[:, lanes].astype(F32)
            stat_parts[to, HEADS + h : HEADS + h + 1, :] = jnp.sum(product.T, axis=0, keepdims=True)
    share = Lane(sends, recvs, 8)
    for flip, step, peer in peers:
        share.send(stat_parts.at[lax.rem(ka + step, KA)], stats.at[c * KA + ka], flip * KA + step, peer)
    keep_stats = pltpu.make_async_copy(stat_parts.at[ka], stats.at[c * KA + ka], local.at[5])
    keep_stats.start()

    key_first.relay_up()
    value_first.relay_up()
    key_then[-1].start()
    value_then[-1].start()
    key_first.relay_down()
    value_first.relay_down()
    key_then[1].start()
    value_then[1].start()
    table[...] = pair_table(z, y, x, c, docs, mask, order)
    keep_table = pltpu.make_async_copy(table, table_out, local.at[11])
    keep_table.start()
    for off in (0,):
        key_then[off].relay_up()
        value_then[off].relay_up()
        key_then[off].relay_down()
        value_then[off].relay_down()
    key_first.finish()
    value_first.finish()
    key_then[2].start()
    value_then[2].start()
    for off in (-1, 1, 2):
        key_then[off].relay_up()
        value_then[off].relay_up()
        key_then[off].relay_down()
        value_then[off].relay_down()
    for off in (0, -1, 1, 2):
        key_then[off].finish()
        value_then[off].finish()

    pair.arrive(sibling_rows.at[0], 0, sibling)
    pair.arrive(sibling_rows.at[1], 1, sibling)
    for flip, step, _ in peers:
        origin = lax.rem(ka + KA - step, KA)
        core = 1 - c if flip else c
        from_ = ident(lax.div(z, 2) * 2 + lax.div(origin, 4), y, lax.rem(origin, 4), core)
        share.arrive(stats.at[core * KA + origin], flip * KA + step, from_)
    keep_stats.wait()
    keep_table.wait()
    for lane in [across, pair, share, key_first, value_first, *key_then.values(), *value_then.values()]:
        lane.drain()


def attend(
    table, stats_in, queries, grad_out, sibling_rows, keys_in, values_in, key_gain, value_gain,
    dq_ref, dk_ref, dv_ref, gains,
    plan, stats, q_ref, g_ref, keys, values, k_ref, v_ref, dk_acc, dv_acc, dq_acc, held, gain_acc, local,
):
    scale = D ** -0.5
    z, _, x, c = place()
    columns = head_columns(z, x)
    own, other = [pl.ds(pl.multiple_of(core * KA * T, KA * T), KA * T) for core in (c, 1 - c)]
    loads = [
        pltpu.make_async_copy(source, target, local.at[n])
        for n, (source, target) in enumerate(
            (
                (keys_in, keys),
                (values_in, values),
                (stats_in, stats),
                (queries.at[:, columns], q_ref.at[own]),
                (grad_out.at[:, columns], g_ref.at[own]),
                (sibling_rows.at[0], q_ref.at[other]),
                (sibling_rows.at[1], g_ref.at[other]),
            )
        )
    ]
    for copy in loads:
        copy.start()
    dk_acc[...] = jnp.zeros_like(dk_acc)
    dv_acc[...] = jnp.zeros_like(dv_acc)
    dq_acc[...] = jnp.zeros_like(dq_acc)

    def stack(ref, i):
        rows = pl.ds(pl.multiple_of(i * T, T), T)
        return jnp.concatenate([ref[rows, h * D : (h + 1) * D] for h in range(HEADS)], axis=0)

    def tiles(ref, a, b):
        parts = [ref[pl.ds(pl.multiple_of(at * T, T), T), :] for at in (a, b)]
        return jnp.concatenate(parts, axis=0)

    def unpack(step):
        word = plan[step]
        return word >> 16, (word >> 8) & 63, word & 63, (word >> 14) & 1, (word >> 6) & 1

    def front(step, slot, masked):
        i, a, b, use_a, use_b = unpack(step)
        s = lax.dot_general(tiles(k_ref, a, b), stack(q_ref, i), NT, preferred_element_type=F32)
        dp = lax.dot_general(tiles(v_ref, a, b), stack(g_ref, i), NT, preferred_element_type=F32)
        lse = jnp.concatenate([stats[i, h : h + 1, :] for h in range(HEADS)], axis=1) * LOG2E
        delta = jnp.concatenate([stats[i, HEADS + h : HEADS + h + 1, :] for h in range(HEADS)], axis=1)
        p = jnp.exp2(s * (scale * LOG2E) - lse)
        if masked:
            row = lax.broadcasted_iota(jnp.int32, (T, T), 0)
            col = lax.broadcasted_iota(jnp.int32, (T, T), 1)
            ok_a = row < use_a * T
            ok_b = row <= col - (1 - use_b) * T
            ok = jnp.concatenate(
                [jnp.concatenate([ok_a] * HEADS, axis=1), jnp.concatenate([ok_b] * HEADS, axis=1)], axis=0
            )
            p = jnp.where(ok, p, 0.0)
        held[slot, 0] = p.astype(BF16)
        held[slot, 1] = (p * (dp - delta)).astype(BF16)

    def back(step, slot):
        i, a, b, _, _ = unpack(step)
        p, ds = held[slot, 0], held[slot, 1]
        dv = jnp.dot(p, stack(g_ref, i), preferred_element_type=F32)
        dk = jnp.dot(ds, stack(q_ref, i), preferred_element_type=F32)
        dq_acc[i] += lax.dot_general(tiles(k_ref, a, b), ds, TN, preferred_element_type=F32)
        for n, at in enumerate((a, b)):
            rows = pl.ds(pl.multiple_of(at * T, T), T)
            dv_acc[rows, :] += dv[n * T : (n + 1) * T]
            dk_acc[rows, :] += dk[n * T : (n + 1) * T]

    def run(steps, masked):
        plan[steps] = 0
        front(0, 0, masked)
        twos = lax.div(steps, 2)

        @pl.loop(0, twos)
        def _(u):
            front(2 * u + 1, 1, masked)
            back(2 * u, 0)
            front(2 * u + 2, 0, masked)
            back(2 * u + 1, 1)

        @pl.when(steps > 2 * twos)
        def _():
            back(steps - 1, 0)

    def list_whole(i, n):
        halves = lax.div(table[i, KEY_TILES], 2)

        def put(r, n):
            plan[n] = (i << 16) | (table[i, 2 * r] << 8) | table[i, 2 * r + 1]
            return n + 1

        return lax.fori_loop(0, halves, put, n)

    steps = lax.fori_loop(0, QUERY_TILES, list_whole, jnp.int32(0))
    lanes = pl.ds(pl.multiple_of(x * D, D), D)
    for n, (raw, scaled, gain) in enumerate(((keys, k_ref, key_gain), (values, v_ref, value_gain))):
        loads[n].wait()
        factor = gain[:, lanes]

        @pl.loop(0, KEY_TILES // 2)
        def _(n):
            at = pl.ds(pl.multiple_of(n * 2 * T, 2 * T), 2 * T)
            scaled[at, :] = (raw[at, :].astype(F32) * factor).astype(BF16)

    for copy in loads[2:]:
        copy.wait()
    run(steps, False)

    def list_masked(i, n):
        count, diag = table[i, KEY_TILES], table[i, KEY_TILES + 1]
        odd = lax.rem(count, 2)
        last = table[i, jnp.maximum(count - 1, 0)]

        @pl.when(odd + diag > 0)
        def _():
            plan[n] = (i << 16) | (odd << 14) | (last << 8) | (diag << 6) | table[i, KEY_TILES + 2]

        return n + jnp.minimum(odd + diag, 1)

    run(lax.fori_loop(0, QUERY_TILES, list_masked, jnp.int32(0)), True)

    @pl.loop(0, QUERY_TILES)
    def _(i):
        rows = pl.ds(pl.multiple_of(i * T, T), T)
        for h in range(HEADS):
            lanes = slice(h * D, (h + 1) * D)
            dq_ref[rows, lanes] = (dq_acc[i, :, lanes].T * scale).astype(BF16)

    gain_acc[...] = jnp.zeros_like(gain_acc)

    @pl.loop(0, KEY_TILES)
    def _(n):
        at = pl.ds(pl.multiple_of(n * T, T), T)
        dkey, dvalue = dk_acc[at, :] * scale, dv_acc[at, :]
        owner = (lax.div(n, 16), lax.rem(lax.div(n, 4), 4), lax.rem(n, 4))
        dk_ref[owner] = dkey.astype(BF16)
        dv_ref[owner] = dvalue.astype(BF16)
        gain_acc[0] += jnp.sum((dkey * keys[at, :].astype(F32)).reshape(T // 8, 8, D), axis=0)
        gain_acc[1] += jnp.sum((dvalue * values[at, :].astype(F32)).reshape(T // 8, 8, D), axis=0)

    gains[...] = jnp.zeros_like(gains)
    for n in range(2):
        gains[n : n + 1, :] = jnp.sum(gain_acc[n], axis=0, keepdims=True)


def scatter(
    dq, dk, dv, partial, key_gain, value_gain,
    grad_queries, grad_keys, grad_values, grad_key_gain, grad_value_gain,
    dq_in, land_z, land_v, land_k, land_zy, land_vz, land_kz, final, near, total, sends, recvs,
):
    z, y, x, c = place()
    ka = lax.rem(z, 2) * 4 + x
    z_hi, z_lo = lax.div(z, 2), lax.rem(z, 2)
    peers = group_peers(z, y, x, c)
    y_plus, y_minus = ident(z, wrap(y + 1), x, c), ident(z, wrap(y - 1), x, c)
    z_plus, z_minus = ident(wrap(z + 1), y, x, c), ident(wrap(z - 1), y, x, c)
    far = ident(wrap(z + 2 * z_lo - 1), y, x, c)
    others = []
    for flip in range(2):
        for step in range(RING):
            if flip or step:
                hi = 1 - z_hi if flip else z_hi
                others.append((flip, step, ident(hi * 2 + z_lo, wrap(y + step), x, c)))
    greet([peer for _, _, peer in peers] + [other for _, _, other in others] + [far])

    spread = Lane(sends, recvs, 70)
    mine = z_hi * RING + y
    for flip, step, other in others:
        spread.send(partial, total.at[mine], flip * RING + step, other)
    total[mine] = partial[...]

    sibling = ident(z, y, x, 1 - c)
    pair = Lane(sends, recvs, 0)
    for n in range(KA):
        rows = pl.ds(pl.multiple_of((1 - c) * KA * T + n * T, T), T)
        pair.send(dq.at[rows], dq_in.at[n], n, sibling)

    z_far, z_near = far, ident(wrap(z + 1 - 2 * z_lo), y, x, c)
    some = pl.ds(0, RING - 1)
    keys_z = Detour(sends, recvs, 16).setup(
        lambda at: dk.at[at, :, some], [pl.ds(0, 2), pl.ds(2, 2)], land_z, z, z_far, z_near
    )
    values_y = Fold(sends, recvs, 22).setup(
        lambda off, n: dv.at[pl.ds(2 * n, 2), wrap(y + off)], land_v, y_plus, y_minus
    )
    last_y = Fold(sends, recvs, 28).setup(
        lambda off, n: dk.at[pl.ds(2 * n, 2), wrap(y + off), RING - 1], land_k, y_plus, y_minus
    )
    keys_z.start()
    last_y.start()
    values_y.start()

    lane_q = Lane(sends, recvs, 8)
    columns = head_columns(z, x)
    for n in range(KA):
        to = lax.rem(ka + n, KA)
        own_rows = dq.at[pl.ds(pl.multiple_of((c * KA + to) * T, T), T)]
        if n == 0:
            for m in range(KA):
                pair.arrive(dq_in.at[m], m, sibling)
        for h in range(HEADS):
            lanes = pl.ds(h * D, D)
            value = own_rows[:, lanes].astype(F32) + dq_in[to, :, lanes].astype(F32)
            dq_in[to, :, lanes] = value.astype(BF16)
        if n:
            peer = ident(z_hi * 2 + lax.div(to, 4), y, lax.rem(to, 4), c)
            lane_q.send(dq_in.at[to], grad_queries.at[:, columns], n, peer)
    grad_queries[:, columns] = dq_in[ka]

    for flip, step, _ in others:
        hi = 1 - z_hi if flip else z_hi
        origin = wrap(y - step)
        spread.arrive(total.at[hi * RING + origin], flip * RING + step, ident(hi * 2 + z_lo, origin, x, c))
    mine = c * KA + ka
    near[mine] = jnp.sum(total[...], axis=0)
    share = Lane(sends, recvs, 54)
    for flip, step, peer in peers:
        share.send(near.at[mine], near.at[mine], flip * KA + step, peer)

    last_y.relay()
    keys_z.relay(0)
    values_y.relay()
    keys_z.relay(1)
    keys_z.finish(land_z.at[1])
    last_y.finish()
    keys_zy = Fold(sends, recvs, 34).setup(
        lambda off, n: land_z.at[1, wrap(y + off), :, pl.ds(n * (T // 2), T // 2)], land_zy, y_plus, y_minus
    )
    keys_zy.start()
    last_yz = Detour(sends, recvs, 44).setup(
        lambda at: land_k.at[2 + lax.div(at, 2), pl.ds(lax.rem(at, 2), 1)], [pl.ds(0, 1)], land_kz, z, z_far, z_near
    )
    last_yz.start()
    values_y.finish()
    values_yz = Detour(sends, recvs, 40).setup(
        lambda at: land_v.at[2 + lax.div(at, 2), lax.rem(at, 2)], [pl.ds(0, RING)], land_vz, z, z_far, z_near
    )
    values_yz.start()
    keys_zy.relay()
    last_yz.relay(0)
    values_yz.relay(0)
    lanes = pl.ds(pl.multiple_of(x * D, D), D)
    key_factor, value_factor = key_gain[:, lanes], value_gain[:, lanes]
    keys_zy.finish(key_factor)
    for n in range(2):
        final[0, 0 : RING - 1, n * (T // 2) : (n + 1) * (T // 2), :] = land_zy[2 + n]
    last_yz.finish(final.at[0, pl.ds(RING - 1, 1)], key_factor)
    values_yz.finish(final.at[1], value_factor)

    across = Lane(sends, recvs, 48)
    for step in range(1, RING):
        to = wrap(x + step)
        across.send(final.at[0, to], grad_keys.at[:, lanes], step - 1, ident(z, y, to, c))
        across.send(final.at[1, to], grad_values.at[:, lanes], step + 2, ident(z, y, to, c))
    grad_keys[:, lanes] = final[0, x]
    grad_values[:, lanes] = final[1, x]

    for flip, step, _ in peers:
        origin = lax.rem(ka + KA - step, KA)
        core = 1 - c if flip else c
        from_ = ident(z_hi * 2 + lax.div(origin, 4), y, lax.rem(origin, 4), core)
        share.arrive(near.at[core * KA + origin], flip * KA + step, from_)
    for n in range(RING):
        whole = near[n] + near[RING + n] + near[2 * RING + n] + near[3 * RING + n]
        grad_key_gain[:, n * D : (n + 1) * D] = whole[0:1]
        grad_value_gain[:, n * D : (n + 1) * D] = whole[1:2]
    for step in range(1, RING):
        origin = wrap(x - step)
        theirs = pl.ds(pl.multiple_of(origin * D, D), D)
        across.arrive(grad_keys.at[:, theirs], step - 1, ident(z, y, origin, c))
        across.arrive(grad_values.at[:, theirs], step + 2, ident(z, y, origin, c))
    for n in range(1, KA):
        origin = lax.rem(ka + KA - n, KA)
        their = head_columns(lax.div(origin, 4), lax.rem(origin, 4))
        from_ = ident(z_hi * 2 + lax.div(origin, 4), y, lax.rem(origin, 4), c)
        lane_q.arrive(grad_queries.at[:, their], n, from_)
    for lane in [
        pair, lane_q, keys_z, values_y, last_y, keys_zy, values_yz, last_yz, across, share, spread
    ]:
        lane.drain()


def shape(dims, dtype):
    return jax.ShapeDtypeStruct(dims, dtype)


def attend_call(table, stats, queries, grad_out, sibling_rows, k, v, key_gain, value_gain):
    vm, hbm = pl.BlockSpec(memory_space=pltpu.VMEM), pl.BlockSpec(memory_space=pl.ANY)
    return pl.pallas_call(
        attend,
        out_shape=(shape((2 * KA * T, WIDTH), BF16), *[shape((RING, RING, RING, T, D), BF16)] * 2, shape((8, D), F32)),
        in_specs=[pl.BlockSpec(memory_space=pltpu.SMEM)] + [hbm] * 6 + [vm] * 2,
        out_specs=(vm,) * 4,
        scratch_shapes=[
            pltpu.SMEM((QUERY_TILES * KEY_TILES // 2 + 2,), jnp.int32),
            pltpu.VMEM(stats.shape, F32),
            pltpu.VMEM((2 * KA * T, WIDTH), BF16),
            pltpu.VMEM((2 * KA * T, WIDTH), BF16),
            pltpu.VMEM(k.shape, BF16),
            pltpu.VMEM(v.shape, BF16),
            pltpu.VMEM(k.shape, BF16),
            pltpu.VMEM(v.shape, BF16),
            pltpu.VMEM(k.shape, F32),
            pltpu.VMEM(v.shape, F32),
            pltpu.VMEM((QUERY_TILES, D, WIDTH), F32),
            pltpu.VMEM((2, 2, 2 * T, WIDTH), BF16),
            pltpu.VMEM((2, 8, D), F32),
            pltpu.SemaphoreType.DMA((7,)),
        ],
        compiler_params=pltpu.CompilerParams(vmem_limit_bytes=47 * 2**20),
        name="attend",
    )(table, stats, queries, grad_out, sibling_rows, k, v, key_gain, value_gain)


def shards(
    queries, key_rows, values, attn_out, grad_out, log_sums, key_gain, value_gain, doc_ids, tile_mask, block_order
):
    vm, hbm = pl.BlockSpec(memory_space=pltpu.VMEM), pl.BlockSpec(memory_space=pl.ANY)
    key_gain, value_gain = key_gain.reshape(1, -1), value_gain.reshape(1, -1)
    rows = queries.shape[0]
    sibling_rows, kg, vg, stats, table = pl.pallas_call(
        gather,
        out_shape=(
            shape((2, rows, WIDTH), BF16),
            shape((RING, RING, RING * T, D), BF16),
            shape((RING, RING, RING * T, D), BF16),
            shape((QUERY_TILES, 2 * HEADS, T), F32),
            shape((QUERY_TILES, T), jnp.int32),
        ),
        in_specs=[hbm] * 9,
        out_specs=(hbm,) * 5,
        scratch_shapes=[
            pltpu.VMEM((QUERY_TILES, T), jnp.int32),
            pltpu.VMEM(attn_out.shape, BF16),
            pltpu.VMEM(log_sums.shape, F32),
            pltpu.VMEM((1, T), jnp.int32),
            pltpu.VMEM(tile_mask.shape, jnp.int32),
            pltpu.VMEM((1, T), jnp.int32),
            pltpu.VMEM(attn_out.shape, BF16),
            pltpu.VMEM((KA, 2 * HEADS, T), F32),
            pltpu.SemaphoreType.DMA((64,)),
            pltpu.SemaphoreType.DMA((64,)),
            pltpu.SemaphoreType.DMA((12,)),
        ],
        compiler_params=pltpu.CompilerParams(
            collective_id=0, has_side_effects=True, vmem_limit_bytes=56 * 2**20
        ),
        name="gather",
    )(
        queries, grad_out, key_rows, values, attn_out, log_sums,
        doc_ids.reshape(1, -1), tile_mask, block_order.reshape(1, -1),
    )
    dq, dk, dv, partial = attend_call(
        table, stats, queries, grad_out, sibling_rows,
        kg.reshape(KEY_TILES * T, D), vg.reshape(KEY_TILES * T, D), key_gain, value_gain,
    )
    grad_queries, grad_keys, grad_values, grad_key_gain, grad_value_gain = pl.pallas_call(
        scatter,
        out_shape=(
            shape(attn_out.shape, BF16),
            shape(key_rows.shape, BF16),
            shape(values.shape, BF16),
            shape(key_gain.shape, F32),
            shape(value_gain.shape, F32),
        ),
        in_specs=[vm] * 6,
        out_specs=(vm,) * 5,
        scratch_shapes=[
            pltpu.VMEM((KA, T, WIDTH), BF16),
            pltpu.VMEM((3, RING, RING - 1, T, D), BF16),
            pltpu.VMEM((6, 2, RING, T, D), BF16),
            pltpu.VMEM((6, 2, T, D), BF16),
            pltpu.VMEM((6, RING - 1, T // 2, D), BF16),
            pltpu.VMEM((3, RING, T, D), BF16),
            pltpu.VMEM((3, 1, T, D), BF16),
            pltpu.VMEM((2, RING, T, D), BF16),
            pltpu.VMEM((QUERY_TILES, 8, D), F32),
            pltpu.VMEM((8, 8, D), F32),
            pltpu.SemaphoreType.DMA((78,)),
            pltpu.SemaphoreType.DMA((78,)),
        ],
        compiler_params=pltpu.CompilerParams(
            collective_id=1, has_side_effects=True, vmem_limit_bytes=20 * 2**20
        ),
        name="scatter",
    )(dq, dk, dv, partial, key_gain, value_gain)
    return grad_queries, grad_keys, grad_values, grad_key_gain.reshape(-1), grad_value_gain.reshape(-1)


def solution(mesh):
    rows = P(("pb", "ka"), None)
    placed = (P("pb", None), rows, rows, rows, P("pb", None), P(None, ("pb", "ka")), P(), P(), P(), P(), P())
    return jax.shard_map(
        shards, mesh=mesh, in_specs=placed, out_specs=(rows, rows, rows, P(), P()), check_vma=False
    )
```

```python
import functools
import math

import jax
import jax.numpy as jnp
from jax import lax
from jax.experimental import pallas as pl
from jax.experimental.pallas import tpu as pltpu
from jax.sharding import PartitionSpec as P


D = 128
T = 128
RING = 4
KA = 8
HEADS = 4
WIDTH = HEADS * D
QUERY_TILES = 16
KEY_TILES = 64
LOG2E = math.log2(math.e)
MESH = pl.DeviceIdType.MESH
F32 = jnp.float32
BF16 = jnp.bfloat16
NT = (((1,), (1,)), ((), ()))
TN = (((0,), (0,)), ((), ()))


def wrap(at):
    return lax.rem(at + RING, RING)


def place():
    pb, ka = lax.axis_index("pb"), lax.axis_index("ka")
    z = lax.div(pb, 8) * 2 + lax.div(ka, 4)
    return z, lax.rem(lax.div(pb, 2), 4), lax.rem(ka, 4), lax.rem(pb, 2)


def ident(z, y, x, c):
    return (lax.div(z, 2) * 8 + y * 2 + c, lax.rem(z, 2) * 4 + x)


def group_peers(z, y, x, c):
    ka = lax.rem(z, 2) * 4 + x
    peers = []
    for flip in range(2):
        for step in range(KA):
            if flip or step:
                to = lax.rem(ka + step, KA)
                core = 1 - c if flip else c
                peers.append((flip, step, ident(lax.div(z, 2) * 2 + lax.div(to, 4), y, lax.rem(to, 4), core)))
    return peers


def greet(devices):
    barrier = pltpu.get_barrier_semaphore()
    for device in devices:
        pl.semaphore_signal(barrier, inc=1, device_id=device, device_id_type=MESH)
    pl.semaphore_wait(barrier, len(devices))


class Lane:
    def __init__(self, sends, recvs, base):
        self.sends, self.recvs, self.base, self.out = sends, recvs, base, []

    def send(self, source, target, number, device):
        copy = pltpu.make_async_remote_copy(
            src_ref=source,
            dst_ref=target,
            send_sem=self.sends.at[self.base + number],
            recv_sem=self.recvs.at[self.base + number],
            device_id=device,
            device_id_type=MESH,
        )
        copy.start()
        self.out.append(copy)

    def arrive(self, target, number, device):
        pltpu.make_async_remote_copy(
            src_ref=target,
            dst_ref=target,
            send_sem=self.sends.at[self.base + number],
            recv_sem=self.recvs.at[self.base + number],
            device_id=device,
            device_id_type=MESH,
        ).wait_recv()

    def drain(self):
        for copy in self.out:
            copy.wait_send()
        self.out = []


class Spread(Lane):
    def setup(self, item, plus, minus):
        self.item, self.plus, self.minus = item, plus, minus
        half = item(0).shape[0] // 2
        self.first, self.second = pl.ds(0, half), pl.ds(half, half)
        return self

    def start(self):
        self.send(self.item(0), self.item(0), 0, self.plus)
        self.send(self.item(0), self.item(0), 1, self.minus)

    def relay_up(self):
        block = self.item(-1)
        self.arrive(block, 0, self.minus)
        self.send(block.at[self.first], block.at[self.first], 2, self.plus)

    def relay_down(self):
        block = self.item(1)
        self.arrive(block, 1, self.plus)
        self.send(block.at[self.second], block.at[self.second], 3, self.minus)

    def finish(self):
        block = self.item(2)
        self.arrive(block.at[self.first], 2, self.minus)
        self.arrive(block.at[self.second], 3, self.plus)


class Fold(Lane):
    def setup(self, half_of, land, plus, minus):
        self.half_of, self.land, self.plus, self.minus = half_of, land, plus, minus
        return self

    def start(self):
        self.send(self.half_of(2, 0), self.land.at[0], 0, self.plus)
        self.send(self.half_of(2, 1), self.land.at[1], 1, self.minus)
        self.send(self.half_of(1, 1), self.land.at[3], 3, self.plus)
        self.send(self.half_of(-1, 0), self.land.at[4], 4, self.minus)

    def relay(self):
        self.arrive(self.land.at[0], 0, self.minus)
        combine(self.land.at[0], [self.land.at[0], self.half_of(1, 0)])
        self.send(self.land.at[0], self.land.at[2], 2, self.plus)
        self.arrive(self.land.at[1], 1, self.plus)
        combine(self.land.at[1], [self.land.at[1], self.half_of(-1, 1)])
        self.send(self.land.at[1], self.land.at[5], 5, self.minus)

    def finish(self, totals):
        self.arrive(self.land.at[3], 3, self.minus)
        self.arrive(self.land.at[4], 4, self.plus)
        self.arrive(self.land.at[2], 2, self.minus)
        combine(totals[0], [self.half_of(0, 0), self.land.at[2], self.land.at[4]])
        self.arrive(self.land.at[5], 5, self.plus)
        combine(totals[1], [self.half_of(0, 1), self.land.at[3], self.land.at[5]])


class Detour(Lane):
    def setup(self, item, cuts, land, z, hi, lo):
        self.item, self.cuts, self.land, self.z, self.hi, self.lo = item, cuts, land, z, hi, lo
        side = 2 * lax.rem(z, 2) - 1
        self.at_hi, self.at_lo, self.at_far = wrap(z + side), wrap(z - side), wrap(z + 2)
        return self

    def start(self):
        for n, cut in enumerate(self.cuts):
            self.send(self.item(self.at_far).at[cut], self.land.at[0].at[cut], n, self.hi)
        self.send(self.item(self.at_hi), self.land.at[1], len(self.cuts), self.hi)

    def relay(self, n):
        cut = self.cuts[n]
        passed = self.land.at[0].at[cut]
        self.arrive(passed, n, self.hi)
        combine(passed, [passed, self.item(self.at_lo).at[cut]])
        self.send(passed, self.land.at[2].at[cut], len(self.cuts) + 1 + n, self.lo)

    def finish(self, total):
        self.arrive(self.land.at[1], len(self.cuts), self.hi)
        for n, cut in enumerate(self.cuts):
            self.arrive(self.land.at[2].at[cut], len(self.cuts) + 1 + n, self.lo)
        combine(total, [self.item(self.z), self.land.at[1], self.land.at[2]])


def combine(total, terms):
    lead = total.shape[:-2]

    @pl.loop(0, math.prod(lead))
    def _(n):
        at = []
        for extent in reversed(lead):
            at.append(lax.rem(n, extent))
            n = lax.div(n, extent)
        at = tuple(reversed(at))
        value = terms[0][at].astype(F32)
        for term in terms[1:]:
            value = value + term[at].astype(F32)
        total[at] = value.astype(total.dtype)


def head_columns(z, x):
    return pl.ds(pl.multiple_of((lax.rem(z, 2) * 4 + x * 8) * D, WIDTH), WIDTH)


def pair_table(z, y, x, c, docs, mask, order):
    z_hi = lax.div(z, 2)
    row = lax.broadcasted_iota(jnp.int32, (T, T), 0)
    col = lax.broadcasted_iota(jnp.int32, (T, T), 1)
    doc_cols = jnp.broadcast_to(docs[...].astype(F32), (T, T))
    live = (mask[...] == 1) & (doc_cols.T == doc_cols) & (row >= col)
    live = jnp.where(live, 1.0, 0.0).astype(BF16)
    holds = jnp.where(row == jnp.broadcast_to(order[...], (T, T)), 1.0, 0.0).astype(BF16)
    by_key = jnp.dot(live, holds, preferred_element_type=F32).astype(BF16)
    stored = lax.dot_general(holds, by_key, TN, preferred_element_type=F32).astype(BF16)
    small_row = lax.broadcasted_iota(jnp.int32, (QUERY_TILES, T), 0)
    small_col = lax.broadcasted_iota(jnp.int32, (QUERY_TILES, T), 1)
    first = (z_hi * 4 + y) * QUERY_TILES
    pick = jnp.where(small_col == small_row + first, 1.0, 0.0).astype(BF16)
    mine = jnp.dot(pick, stored, preferred_element_type=F32).astype(BF16)
    slot_z, slot_y, slot_x = col // 16, col // 4 % 4, col % 4
    source = (slot_z // 2) * 64 + slot_y * 16 + c * 8 + slot_z % 2 * 4 + slot_x
    spread = jnp.where((row == source) & (col < KEY_TILES), 1.0, 0.0).astype(BF16)
    pairs = jnp.dot(mine, spread, preferred_element_type=F32)
    own = ((z_hi * 2 + small_row % 8 // 4) * 4 + y) * 4 + small_row % 4
    is_own = (small_col == own) & (small_row // 8 == c)
    diag = jnp.sum(jnp.where(is_own, pairs, 0.0), axis=1, keepdims=True)
    rest = jnp.where(is_own, 0.0, pairs)
    upto = jnp.where(row <= col, 1.0, 0.0).astype(BF16)
    rank = jnp.dot(rest.astype(BF16), upto, preferred_element_type=F32)
    count = jnp.sum(rest, axis=1, keepdims=True)
    numbers = lax.broadcasted_iota(jnp.int32, (8, T), 1).astype(F32).astype(BF16)
    lists = []
    for i in range(QUERY_TILES):
        at = jnp.where(rest[i : i + 1, :] > 0.5, rank[i : i + 1, :] - 1.0, -1.0)
        chosen = jnp.where(jnp.broadcast_to(at, (T, T)) == row.astype(F32), 1.0, 0.0).astype(BF16)
        lists.append(lax.dot_general(numbers, chosen, NT, preferred_element_type=F32)[:1])
    table = jnp.concatenate(lists, axis=0)
    table = jnp.where(small_col == KEY_TILES, count, table)
    table = jnp.where(small_col == KEY_TILES + 1, diag, table)
    table = table.astype(jnp.int32)
    return jnp.where(small_col == KEY_TILES + 2, jnp.where(small_row // 8 == c, own, 0), table)


def gather(
    queries, grad_out, keys, values, attn_in, logs_in, docs_in, mask_in, order_in,
    sibling_rows, kg, vg, stats, table_out,
    table, attn_out, log_sums, docs, mask, order,
    own_grad, stat_parts, sends, recvs, local,
):
    z, y, x, c = place()
    ka = lax.rem(z, 2) * 4 + x
    columns = head_columns(z, x)
    own_rows = pl.ds(pl.multiple_of(ka * T, T), T)
    loads = [
        pltpu.make_async_copy(source, target, local.at[6 + n])
        for n, (source, target) in enumerate(
            (
                (attn_in, attn_out),
                (logs_in, log_sums),
                (docs_in, docs),
                (mask_in, mask),
                (order_in, order),
            )
        )
    ]
    loads.append(pltpu.make_async_copy(grad_out.at[own_rows], own_grad, local.at[0]))
    for copy in loads:
        copy.start()

    def part(ref, to):
        return ref.at[:, pl.ds(pl.multiple_of(to * D, D), D)]

    peers = group_peers(z, y, x, c)
    y_plus, y_minus = ident(z, wrap(y + 1), x, c), ident(z, wrap(y - 1), x, c)
    z_plus, z_minus = ident(wrap(z + 1), y, x, c), ident(wrap(z - 1), y, x, c)
    far = ident(wrap(z + 2 * lax.rem(z, 2) - 1), y, x, c)
    greet([peer for _, _, peer in peers] + [y_plus, y_minus, far])

    slot = pl.ds(pl.multiple_of(x * T, T), T)
    across = Lane(sends, recvs, 0)
    for step in range(1, RING):
        to = wrap(x + step)
        across.send(part(keys, to), kg.at[z, y, slot], step - 1, ident(z, y, to, c))
        across.send(part(values, to), vg.at[z, y, slot], step + 2, ident(z, y, to, c))
    kept = [
        pltpu.make_async_copy(part(keys, x), kg.at[z, y, slot], local.at[3]),
        pltpu.make_async_copy(part(values, x), vg.at[z, y, slot], local.at[4]),
    ]
    for copy in kept:
        copy.start()
    sibling = ident(z, y, x, 1 - c)
    pair = Lane(sends, recvs, 6)
    pair.send(queries.at[:, columns], sibling_rows.at[0], 0, sibling)
    pair.send(grad_out.at[:, columns], sibling_rows.at[1], 1, sibling)

    for copy in kept:
        copy.wait()
    for step in range(1, RING):
        origin = wrap(x - step)
        came = pl.ds(pl.multiple_of(origin * T, T), T)
        across.arrive(kg.at[z, y, came], step - 1, ident(z, y, origin, c))
        across.arrive(vg.at[z, y, came], step + 2, ident(z, y, origin, c))

    def block(ref, dz, dy):
        return ref.at[wrap(z + dz), wrap(y + dy)]

    base = 24
    key_first = Spread(sends, recvs, base).setup(lambda o: block(kg, o, 0), z_plus, z_minus)
    value_first = Spread(sends, recvs, base + 4).setup(lambda o: block(vg, 0, o), y_plus, y_minus)
    key_then, value_then = {}, {}
    for n, off in enumerate((0, -1, 1, 2)):
        key_then[off] = Spread(sends, recvs, base + 8 + 4 * n).setup(
            lambda o, off=off: block(kg, off, o), y_plus, y_minus
        )
        value_then[off] = Spread(sends, recvs, base + 24 + 4 * n).setup(
            lambda o, off=off: block(vg, o, off), z_plus, z_minus
        )
    key_first.start()
    value_first.start()
    key_then[0].start()
    value_then[0].start()

    for copy in loads:
        copy.wait()
    for to in range(KA):
        first = to % 4 * 8 + to // 4 * 4
        stat_parts[to, 0:HEADS, :] = log_sums[first : first + HEADS, :]
        for h in range(HEADS):
            lanes = pl.ds((first + h) * D, D)
            product = own_grad[:, lanes].astype(F32) * attn_out[:, lanes].astype(F32)
            stat_parts[to, HEADS + h : HEADS + h + 1, :] = jnp.sum(product.T, axis=0, keepdims=True)
    share = Lane(sends, recvs, 8)
    for flip, step, peer in peers:
        share.send(stat_parts.at[lax.rem(ka + step, KA)], stats.at[c * KA + ka], flip * KA + step, peer)
    keep_stats = pltpu.make_async_copy(stat_parts.at[ka], stats.at[c * KA + ka], local.at[5])
    keep_stats.start()

    key_first.relay_up()
    value_first.relay_up()
    key_then[-1].start()
    value_then[-1].start()
    key_first.relay_down()
    value_first.relay_down()
    key_then[1].start()
    value_then[1].start()
    table[...] = pair_table(z, y, x, c, docs, mask, order)
    keep_table = pltpu.make_async_copy(table, table_out, local.at[11])
    keep_table.start()
    for off in (0,):
        key_then[off].relay_up()
        value_then[off].relay_up()
        key_then[off].relay_down()
        value_then[off].relay_down()
    key_first.finish()
    value_first.finish()
    key_then[2].start()
    value_then[2].start()
    for off in (-1, 1, 2):
        key_then[off].relay_up()
        value_then[off].relay_up()
        key_then[off].relay_down()
        value_then[off].relay_down()
    for off in (0, -1, 1, 2):
        key_then[off].finish()
        value_then[off].finish()

    pair.arrive(sibling_rows.at[0], 0, sibling)
    pair.arrive(sibling_rows.at[1], 1, sibling)
    for flip, step, _ in peers:
        origin = lax.rem(ka + KA - step, KA)
        core = 1 - c if flip else c
        from_ = ident(lax.div(z, 2) * 2 + lax.div(origin, 4), y, lax.rem(origin, 4), core)
        share.arrive(stats.at[core * KA + origin], flip * KA + step, from_)
    keep_stats.wait()
    keep_table.wait()
    for lane in [across, pair, share, key_first, value_first, *key_then.values(), *value_then.values()]:
        lane.drain()


def attend(
    table, stats_in, queries, grad_out, sibling_rows, keys_in, values_in, key_gain, value_gain,
    dq_ref, dk_ref, dv_ref, gains,
    plan, stats, q_ref, g_ref, keys, values, k_ref, v_ref, dk_acc, dv_acc, dq_acc, held, gain_acc, local,
):
    scale = D ** -0.5
    z, _, x, c = place()
    columns = head_columns(z, x)
    own, other = [pl.ds(pl.multiple_of(core * KA * T, KA * T), KA * T) for core in (c, 1 - c)]
    loads = [
        pltpu.make_async_copy(source, target, local.at[n])
        for n, (source, target) in enumerate(
            (
                (keys_in, keys),
                (values_in, values),
                (stats_in, stats),
                (queries.at[:, columns], q_ref.at[own]),
                (grad_out.at[:, columns], g_ref.at[own]),
                (sibling_rows.at[0], q_ref.at[other]),
                (sibling_rows.at[1], g_ref.at[other]),
            )
        )
    ]
    for copy in loads:
        copy.start()
    dk_acc[...] = jnp.zeros_like(dk_acc)
    dv_acc[...] = jnp.zeros_like(dv_acc)
    dq_acc[...] = jnp.zeros_like(dq_acc)

    def stack(ref, i):
        rows = pl.ds(pl.multiple_of(i * T, T), T)
        return jnp.concatenate([ref[rows, h * D : (h + 1) * D] for h in range(HEADS)], axis=0)

    def tiles(ref, a, b):
        parts = [ref[pl.ds(pl.multiple_of(at * T, T), T), :] for at in (a, b)]
        return jnp.concatenate(parts, axis=0)

    def unpack(step):
        word = plan[step]
        return word >> 16, (word >> 8) & 63, word & 63, (word >> 14) & 1, (word >> 6) & 1

    def front(step, slot, masked):
        i, a, b, use_a, use_b = unpack(step)
        s = lax.dot_general(tiles(k_ref, a, b), stack(q_ref, i), NT, preferred_element_type=F32)
        dp = lax.dot_general(tiles(v_ref, a, b), stack(g_ref, i), NT, preferred_element_type=F32)
        lse = jnp.concatenate([stats[i, h : h + 1, :] for h in range(HEADS)], axis=1) * LOG2E
        delta = jnp.concatenate([stats[i, HEADS + h : HEADS + h + 1, :] for h in range(HEADS)], axis=1)
        p = jnp.exp2(s * (scale * LOG2E) - lse)
        if masked:
            row = lax.broadcasted_iota(jnp.int32, (T, T), 0)
            col = lax.broadcasted_iota(jnp.int32, (T, T), 1)
            ok_a = row < use_a * T
            ok_b = row <= col - (1 - use_b) * T
            ok = jnp.concatenate(
                [jnp.concatenate([ok_a] * HEADS, axis=1), jnp.concatenate([ok_b] * HEADS, axis=1)], axis=0
            )
            p = jnp.where(ok, p, 0.0)
        held[slot, 0] = p.astype(BF16)
        held[slot, 1] = (p * (dp - delta)).astype(BF16)

    def back(step, slot):
        i, a, b, _, _ = unpack(step)
        p, ds = held[slot, 0], held[slot, 1]
        dv = jnp.dot(p, stack(g_ref, i), preferred_element_type=F32)
        dk = jnp.dot(ds, stack(q_ref, i), preferred_element_type=F32)
        dq_acc[i] += lax.dot_general(tiles(k_ref, a, b), ds, TN, preferred_element_type=F32)
        for n, at in enumerate((a, b)):
            rows = pl.ds(pl.multiple_of(at * T, T), T)
            dv_acc[rows, :] += dv[n * T : (n + 1) * T]
            dk_acc[rows, :] += dk[n * T : (n + 1) * T]

    def run(steps, masked, unroll):
        plan[steps] = 0
        front(0, 0, masked)

        def twos(first, count):
            for r in range(0, count, 2):
                front(first + r + 1, 1, masked)
                back(first + r, 0)
                front(first + r + 2, 0, masked)
                back(first + r + 1, 1)

        whole = lax.div(steps, unroll)

        @pl.loop(0, whole)
        def _(u):
            twos(u * unroll, unroll)

        if unroll > 2:

            @pl.loop(whole * (unroll // 2), lax.div(steps, 2))
            def _(u):
                twos(2 * u, 2)

        @pl.when(lax.rem(steps, 2) > 0)
        def _():
            back(steps - 1, 0)

    def list_whole(i, n):
        halves = lax.div(table[i, KEY_TILES], 2)

        def put(r, n):
            plan[n] = (i << 16) | (table[i, 2 * r] << 8) | table[i, 2 * r + 1]
            return n + 1

        return lax.fori_loop(0, halves, put, n)

    steps = lax.fori_loop(0, QUERY_TILES, list_whole, jnp.int32(0))
    lanes = pl.ds(pl.multiple_of(x * D, D), D)
    for n, (raw, scaled, gain) in enumerate(((keys, k_ref, key_gain), (values, v_ref, value_gain))):
        loads[n].wait()
        factor = gain[:, lanes]

        @pl.loop(0, KEY_TILES // 2)
        def _(n):
            at = pl.ds(pl.multiple_of(n * 2 * T, 2 * T), 2 * T)
            scaled[at, :] = (raw[at, :].astype(F32) * factor).astype(BF16)

    for copy in loads[2:]:
        copy.wait()
    run(steps, False, 8)

    def list_masked(i, n):
        count, diag = table[i, KEY_TILES], table[i, KEY_TILES + 1]
        odd = lax.rem(count, 2)
        last = table[i, jnp.maximum(count - 1, 0)]

        @pl.when(odd + diag > 0)
        def _():
            plan[n] = (i << 16) | (odd << 14) | (last << 8) | (diag << 6) | table[i, KEY_TILES + 2]

        return n + jnp.minimum(odd + diag, 1)

    run(lax.fori_loop(0, QUERY_TILES, list_masked, jnp.int32(0)), True, 2)

    @pl.loop(0, QUERY_TILES)
    def _(i):
        rows = pl.ds(pl.multiple_of(i * T, T), T)
        for h in range(HEADS):
            lanes = slice(h * D, (h + 1) * D)
            dq_ref[rows, lanes] = (dq_acc[i, :, lanes].T * scale).astype(BF16)

    gain_acc[...] = jnp.zeros_like(gain_acc)

    @pl.loop(0, KEY_TILES)
    def _(n):
        at = pl.ds(pl.multiple_of(n * T, T), T)
        dkey, dvalue = dk_acc[at, :] * scale, dv_acc[at, :]
        owner = (lax.div(n, 16), lax.rem(lax.div(n, 4), 4), lax.rem(n, 4))
        dk_ref[owner] = dkey.astype(BF16)
        dv_ref[owner] = dvalue.astype(BF16)
        gain_acc[0] += jnp.sum((dkey * keys[at, :].astype(F32)).reshape(T // 8, 8, D), axis=0)
        gain_acc[1] += jnp.sum((dvalue * values[at, :].astype(F32)).reshape(T // 8, 8, D), axis=0)

    gains[...] = jnp.zeros_like(gains)
    for n in range(2):
        gains[n : n + 1, :] = jnp.sum(gain_acc[n], axis=0, keepdims=True)


def scatter(
    dq, dk, dv, partial, key_gain, value_gain,
    grad_queries, grad_keys, grad_values, grad_key_gain, grad_value_gain,
    dq_in, land_z, land_v, land_k, out_k, out_v, in_k, in_v, near, total, sends, recvs,
):
    z, y, x, c = place()
    ka = lax.rem(z, 2) * 4 + x
    z_hi, z_lo = lax.div(z, 2), lax.rem(z, 2)
    y_plus, y_minus = ident(z, wrap(y + 1), x, c), ident(z, wrap(y - 1), x, c)
    z_far, z_near = ident(wrap(z + 2 * z_lo - 1), y, x, c), ident(wrap(z + 1 - 2 * z_lo), y, x, c)
    steps = [(one, two) for one in range(RING) for two in range(RING) if one or two]
    in_y = [ident(z, wrap(y + one), wrap(x + two), c) for one, two in steps]
    in_z = [ident(wrap(z + one), y, wrap(x + two), c) for one, two in steps]
    others = [(0, one, ident(wrap(z + one), y, x, c)) for one in range(1, RING)]
    others += [(1, one, ident(wrap(z + one), y, x, 1 - c)) for one in range(RING)]
    greet(in_y + [peer for peer, (one, _) in zip(in_z, steps) if one] + [other for flip, _, other in others if flip])

    spread = Lane(sends, recvs, 88)
    for (one, two), peer in zip(steps, in_y):
        spread.send(partial, near.at[one, two], one * RING + two, peer)
    near[0, 0] = partial[...]

    sibling = ident(z, y, x, 1 - c)
    pair = Lane(sends, recvs, 0)
    for n in range(KA):
        rows = pl.ds(pl.multiple_of((1 - c) * KA * T + n * T, T), T)
        pair.send(dq.at[rows], dq_in.at[n], n, sibling)

    keys_z = Detour(sends, recvs, 16).setup(
        lambda at: dk.at[at, :, pl.ds(0, RING - 1)], [pl.ds(0, 2), pl.ds(2, 2)], land_z, z, z_far, z_near
    )
    last_y = Fold(sends, recvs, 22).setup(
        lambda off, n: dk.at[pl.ds(2 * n, 2), wrap(y + off), pl.ds(RING - 1, 1)], land_k, y_plus, y_minus
    )
    rows_of = [pl.ds(n * (T // 2), T // 2) for n in range(2)]
    values_y = [
        Fold(sends, recvs, 28 + 6 * part).setup(
            lambda off, n, rows=rows: dv.at[pl.ds(2 * n, 2), wrap(y + off), :, rows], land_v.at[part], y_plus, y_minus
        )
        for part, rows in enumerate(rows_of)
    ]
    keys_z.start()
    last_y.start()
    values_y[0].start()
    values_y[1].start()

    lane_q = Lane(sends, recvs, 8)
    columns = head_columns(z, x)
    for n in range(KA):
        to = lax.rem(ka + n, KA)
        own_rows = dq.at[pl.ds(pl.multiple_of((c * KA + to) * T, T), T)]
        if n == 0:
            for m in range(KA):
                pair.arrive(dq_in.at[m], m, sibling)
        for h in range(HEADS):
            lanes = pl.ds(h * D, D)
            value = own_rows[:, lanes].astype(F32) + dq_in[to, :, lanes].astype(F32)
            dq_in[to, :, lanes] = value.astype(BF16)
        if n:
            peer = ident(z_hi * 2 + lax.div(to, 4), y, lax.rem(to, 4), c)
            lane_q.send(dq_in.at[to], grad_queries.at[:, columns], n, peer)
    grad_queries[:, columns] = dq_in[ka]

    for (one, two), peer in zip(steps, in_y):
        spread.arrive(near.at[one, two], one * RING + two, peer)
    for n in range(RING):
        block = near[wrap(y), wrap(x - n + RING)]
        for one in range(1, RING):
            block = block + near[wrap(y - one + RING), wrap(x - n + RING)]
        total[0, 2 * n : 2 * n + 2, :] = block[0:2]
    mine = c * RING + z
    total[1 + mine] = total[0]
    share = Lane(sends, recvs, 104)
    for flip, step, other in others:
        share.send(total.at[0], total.at[1 + mine], flip * RING + step, other)

    last_y.relay()
    keys_z.relay(0)
    values_y[0].relay()
    keys_z.relay(1)
    last_y.finish([out_k.at[pl.ds(2 * n, 2), pl.ds(RING - 1, 1)] for n in range(2)])
    values_y[0].finish([out_v.at[pl.ds(2 * n, 2), :, rows_of[0]] for n in range(2)])

    def send_values(part):
        lane = Lane(sends, recvs, 56 + 16 * part)
        for (one, two), peer in zip(steps, in_z):
            block = out_v.at[wrap(z + one), wrap(x + two), rows_of[part]]
            lane.send(block, in_v.at[one, two, rows_of[part]], one * RING + two, peer)
        return lane

    values_out = [send_values(0)]
    values_y[1].relay()
    keys_z.finish(out_k.at[:, pl.ds(0, RING - 1)])
    keys_out = Lane(sends, recvs, 40)
    for one, two in steps:
        to = wrap(x + two)
        over_z = lax.div(to, RING - 1)
        to_z, to_y = wrap(z + one * over_z), wrap(y + one * (1 - over_z))
        block = out_k.at[over_z * to_z + (1 - over_z) * to_y, to]
        keys_out.send(block, in_k.at[one, two], one * RING + two, ident(to_z, to_y, to, c))
    values_y[1].finish([out_v.at[pl.ds(2 * n, 2), :, rows_of[1]] for n in range(2)])
    values_out.append(send_values(1))

    def deliver(result, gain, own, came):
        for two in range(RING):
            lanes = pl.ds(pl.multiple_of(wrap(x - two) * D, D), D)
            value = (own if two == 0 else came[0, two]).astype(F32)
            for one in range(1, RING):
                value = value + came[one, two].astype(F32)
            result[:, lanes] = (value * gain[:, lanes]).astype(BF16)

    for (one, two), peer in zip(steps, in_y):
        keys_out.arrive(in_k.at[one, two], one * RING + two, peer)
    own_over_z = lax.div(x, RING - 1)
    deliver(grad_keys, key_gain, out_k[own_over_z * z + (1 - own_over_z) * y, x], in_k)
    for part in range(2):
        for (one, two), peer in zip(steps, in_z):
            values_out[part].arrive(in_v.at[one, two, rows_of[part]], one * RING + two, peer)
    deliver(grad_values, value_gain, out_v[z, x], in_v)

    for flip, step, other in others:
        origin = (1 - c if flip else c) * RING + wrap(z - step)
        share.arrive(total.at[1 + origin], flip * RING + step, other)
    whole = jnp.sum(total[1:], axis=0)
    for n in range(RING):
        grad_key_gain[:, n * D : (n + 1) * D] = whole[2 * n : 2 * n + 1]
        grad_value_gain[:, n * D : (n + 1) * D] = whole[2 * n + 1 : 2 * n + 2]
    for n in range(1, KA):
        origin = lax.rem(ka + KA - n, KA)
        their = head_columns(lax.div(origin, 4), lax.rem(origin, 4))
        from_ = ident(z_hi * 2 + lax.div(origin, 4), y, lax.rem(origin, 4), c)
        lane_q.arrive(grad_queries.at[:, their], n, from_)
    for lane in [
        pair, lane_q, keys_z, last_y, *values_y, keys_out, *values_out, share, spread
    ]:
        lane.drain()


def shape(dims, dtype):
    return jax.ShapeDtypeStruct(dims, dtype)


def attend_call(table, stats, queries, grad_out, sibling_rows, k, v, key_gain, value_gain):
    vm, hbm = pl.BlockSpec(memory_space=pltpu.VMEM), pl.BlockSpec(memory_space=pl.ANY)
    return pl.pallas_call(
        attend,
        out_shape=(shape((2 * KA * T, WIDTH), BF16), *[shape((RING, RING, RING, T, D), BF16)] * 2, shape((8, D), F32)),
        in_specs=[pl.BlockSpec(memory_space=pltpu.SMEM)] + [hbm] * 6 + [vm] * 2,
        out_specs=(vm,) * 4,
        scratch_shapes=[
            pltpu.SMEM((QUERY_TILES * KEY_TILES // 2 + 2,), jnp.int32),
            pltpu.VMEM(stats.shape, F32),
            pltpu.VMEM((2 * KA * T, WIDTH), BF16),
            pltpu.VMEM((2 * KA * T, WIDTH), BF16),
            pltpu.VMEM(k.shape, BF16),
            pltpu.VMEM(v.shape, BF16),
            pltpu.VMEM(k.shape, BF16),
            pltpu.VMEM(v.shape, BF16),
            pltpu.VMEM(k.shape, F32),
            pltpu.VMEM(v.shape, F32),
            pltpu.VMEM((QUERY_TILES, D, WIDTH), F32),
            pltpu.VMEM((2, 2, 2 * T, WIDTH), BF16),
            pltpu.VMEM((2, 8, D), F32),
            pltpu.SemaphoreType.DMA((7,)),
        ],
        compiler_params=pltpu.CompilerParams(vmem_limit_bytes=47 * 2**20),
        name="attend",
    )(table, stats, queries, grad_out, sibling_rows, k, v, key_gain, value_gain)


def shards(
    queries, key_rows, values, attn_out, grad_out, log_sums, key_gain, value_gain, doc_ids, tile_mask, block_order
):
    vm, hbm = pl.BlockSpec(memory_space=pltpu.VMEM), pl.BlockSpec(memory_space=pl.ANY)
    key_gain, value_gain = key_gain.reshape(1, -1), value_gain.reshape(1, -1)
    rows = queries.shape[0]
    sibling_rows, kg, vg, stats, table = pl.pallas_call(
        gather,
        out_shape=(
            shape((2, rows, WIDTH), BF16),
            shape((RING, RING, RING * T, D), BF16),
            shape((RING, RING, RING * T, D), BF16),
            shape((QUERY_TILES, 2 * HEADS, T), F32),
            shape((QUERY_TILES, T), jnp.int32),
        ),
        in_specs=[hbm] * 9,
        out_specs=(hbm,) * 5,
        scratch_shapes=[
            pltpu.VMEM((QUERY_TILES, T), jnp.int32),
            pltpu.VMEM(attn_out.shape, BF16),
            pltpu.VMEM(log_sums.shape, F32),
            pltpu.VMEM((1, T), jnp.int32),
            pltpu.VMEM(tile_mask.shape, jnp.int32),
            pltpu.VMEM((1, T), jnp.int32),
            pltpu.VMEM(attn_out.shape, BF16),
            pltpu.VMEM((KA, 2 * HEADS, T), F32),
            pltpu.SemaphoreType.DMA((64,)),
            pltpu.SemaphoreType.DMA((64,)),
            pltpu.SemaphoreType.DMA((12,)),
        ],
        compiler_params=pltpu.CompilerParams(
            collective_id=0, has_side_effects=True, vmem_limit_bytes=56 * 2**20
        ),
        name="gather",
    )(
        queries, grad_out, key_rows, values, attn_out, log_sums,
        doc_ids.reshape(1, -1), tile_mask, block_order.reshape(1, -1),
    )
    dq, dk, dv, partial = attend_call(
        table, stats, queries, grad_out, sibling_rows,
        kg.reshape(KEY_TILES * T, D), vg.reshape(KEY_TILES * T, D), key_gain, value_gain,
    )
    grad_queries, grad_keys, grad_values, grad_key_gain, grad_value_gain = pl.pallas_call(
        scatter,
        out_shape=(
            shape(attn_out.shape, BF16),
            shape(key_rows.shape, BF16),
            shape(values.shape, BF16),
            shape(key_gain.shape, F32),
            shape(value_gain.shape, F32),
        ),
        in_specs=[vm] * 6,
        out_specs=(vm,) * 5,
        scratch_shapes=[
            pltpu.VMEM((KA, T, WIDTH), BF16),
            pltpu.VMEM((3, RING, RING - 1, T, D), BF16),
            pltpu.VMEM((2, 6, 2, RING, T // 2, D), BF16),
            pltpu.VMEM((6, 2, 1, T, D), BF16),
            pltpu.VMEM((RING, RING, T, D), BF16),
            pltpu.VMEM((RING, RING, T, D), BF16),
            pltpu.VMEM((RING, RING, T, D), BF16),
            pltpu.VMEM((RING, RING, T, D), BF16),
            pltpu.VMEM((RING, RING, 8, D), F32),
            pltpu.VMEM((9, 8, D), F32),
            pltpu.SemaphoreType.DMA((112,)),
            pltpu.SemaphoreType.DMA((112,)),
        ],
        compiler_params=pltpu.CompilerParams(
            collective_id=1, has_side_effects=True, vmem_limit_bytes=20 * 2**20
        ),
        name="scatter",
    )(dq, dk, dv, partial, key_gain, value_gain)
    return grad_queries, grad_keys, grad_values, grad_key_gain.reshape(-1), grad_value_gain.reshape(-1)


def solution(mesh):
    rows = P(("pb", "ka"), None)
    placed = (P("pb", None), rows, rows, rows, P("pb", None), P(None, ("pb", "ka")), P(), P(), P(), P(), P())
    return jax.shard_map(
        shards, mesh=mesh, in_specs=placed, out_specs=(rows, rows, rows, P(), P()), check_vma=False
    )
```

```python
import functools
import math

import jax
import jax.numpy as jnp
from jax import lax
from jax.experimental import pallas as pl
from jax.experimental.pallas import tpu as pltpu
from jax.sharding import PartitionSpec as P


D = 128
T = 128
RING = 4
KA = 8
HEADS = 4
WIDTH = HEADS * D
QUERY_TILES = 16
KEY_TILES = 64
Z_FIRST = 3
PARTS = 2
LOG2E = math.log2(math.e)
MESH = pl.DeviceIdType.MESH
F32 = jnp.float32
BF16 = jnp.bfloat16
NT = (((1,), (1,)), ((), ()))
TN = (((0,), (0,)), ((), ()))


def wrap(at):
    return lax.rem(at + RING, RING)


def place():
    pb, ka = lax.axis_index("pb"), lax.axis_index("ka")
    z = lax.div(pb, 8) * 2 + lax.div(ka, 4)
    return z, lax.rem(lax.div(pb, 2), 4), lax.rem(ka, 4), lax.rem(pb, 2)


def ident(z, y, x, c):
    return (lax.div(z, 2) * 8 + y * 2 + c, lax.rem(z, 2) * 4 + x)


def group_peers(z, y, x, c):
    ka = lax.rem(z, 2) * 4 + x
    peers = []
    for flip in range(2):
        for step in range(KA):
            if flip or step:
                to = lax.rem(ka + step, KA)
                core = 1 - c if flip else c
                peers.append((flip, step, ident(lax.div(z, 2) * 2 + lax.div(to, 4), y, lax.rem(to, 4), core)))
    return peers


def greet(devices):
    barrier = pltpu.get_barrier_semaphore()
    for device in devices:
        pl.semaphore_signal(barrier, inc=1, device_id=device, device_id_type=MESH)
    pl.semaphore_wait(barrier, len(devices))


class Lane:
    def __init__(self, sends, recvs, base):
        self.sends, self.recvs, self.base, self.out = sends, recvs, base, []

    def send(self, source, target, number, device):
        copy = pltpu.make_async_remote_copy(
            src_ref=source,
            dst_ref=target,
            send_sem=self.sends.at[self.base + number],
            recv_sem=self.recvs.at[self.base + number],
            device_id=device,
            device_id_type=MESH,
        )
        copy.start()
        self.out.append(copy)

    def arrive(self, target, number, device):
        pltpu.make_async_remote_copy(
            src_ref=target,
            dst_ref=target,
            send_sem=self.sends.at[self.base + number],
            recv_sem=self.recvs.at[self.base + number],
            device_id=device,
            device_id_type=MESH,
        ).wait_recv()

    def drain(self):
        for copy in self.out:
            copy.wait_send()
        self.out = []


class Spread(Lane):
    def setup(self, item, plus, minus):
        self.item, self.plus, self.minus = item, plus, minus
        half = item(0).shape[0] // 2
        self.first, self.second = pl.ds(0, half), pl.ds(half, half)
        return self

    def start(self):
        self.send(self.item(0), self.item(0), 0, self.plus)
        self.send(self.item(0), self.item(0), 1, self.minus)

    def relay_up(self):
        block = self.item(-1)
        self.arrive(block, 0, self.minus)
        self.send(block.at[self.first], block.at[self.first], 2, self.plus)

    def relay_down(self):
        block = self.item(1)
        self.arrive(block, 1, self.plus)
        self.send(block.at[self.second], block.at[self.second], 3, self.minus)

    def finish(self):
        block = self.item(2)
        self.arrive(block.at[self.first], 2, self.minus)
        self.arrive(block.at[self.second], 3, self.plus)


class Fold(Lane):
    def setup(self, half_of, land, plus, minus):
        self.half_of, self.land, self.plus, self.minus = half_of, land, plus, minus
        return self

    def start(self):
        self.send(self.half_of(2, 0), self.land.at[0], 0, self.plus)
        self.send(self.half_of(2, 1), self.land.at[1], 1, self.minus)
        self.send(self.half_of(1, 1), self.land.at[3], 3, self.plus)
        self.send(self.half_of(-1, 0), self.land.at[4], 4, self.minus)

    def relay(self):
        self.arrive(self.land.at[0], 0, self.minus)
        combine(self.land.at[0], [self.land.at[0], self.half_of(1, 0)])
        self.send(self.land.at[0], self.land.at[2], 2, self.plus)
        self.arrive(self.land.at[1], 1, self.plus)
        combine(self.land.at[1], [self.land.at[1], self.half_of(-1, 1)])
        self.send(self.land.at[1], self.land.at[5], 5, self.minus)

    def finish(self, totals):
        self.arrive(self.land.at[3], 3, self.minus)
        self.arrive(self.land.at[4], 4, self.plus)
        self.arrive(self.land.at[2], 2, self.minus)
        combine(totals[0], [self.half_of(0, 0), self.land.at[2], self.land.at[4]])
        self.arrive(self.land.at[5], 5, self.plus)
        combine(totals[1], [self.half_of(0, 1), self.land.at[3], self.land.at[5]])


class Detour(Lane):
    def setup(self, item, cuts, land, z, hi, lo):
        self.item, self.cuts, self.land, self.z, self.hi, self.lo = item, cuts, land, z, hi, lo
        side = 2 * lax.rem(z, 2) - 1
        self.at_hi, self.at_lo, self.at_far = wrap(z + side), wrap(z - side), wrap(z + 2)
        return self

    def start(self):
        for n, cut in enumerate(self.cuts):
            self.send(self.item(self.at_far).at[cut], self.land.at[0].at[cut], n, self.hi)
        self.send(self.item(self.at_hi), self.land.at[1], len(self.cuts), self.hi)

    def relay(self, n):
        cut = self.cuts[n]
        passed = self.land.at[0].at[cut]
        self.arrive(passed, n, self.hi)
        combine(passed, [passed, self.item(self.at_lo).at[cut]])
        self.send(passed, self.land.at[2].at[cut], len(self.cuts) + 1 + n, self.lo)

    def finish(self, total):
        self.arrive(self.land.at[1], len(self.cuts), self.hi)
        for n, cut in enumerate(self.cuts):
            self.arrive(self.land.at[2].at[cut], len(self.cuts) + 1 + n, self.lo)
        combine(total, [self.item(self.z), self.land.at[1], self.land.at[2]])


def combine(total, terms):
    lead = total.shape[:-2]

    @pl.loop(0, math.prod(lead))
    def _(n):
        at = []
        for extent in reversed(lead):
            at.append(lax.rem(n, extent))
            n = lax.div(n, extent)
        at = tuple(reversed(at))
        value = terms[0][at].astype(F32)
        for term in terms[1:]:
            value = value + term[at].astype(F32)
        total[at] = value.astype(total.dtype)


def head_columns(z, x):
    return pl.ds(pl.multiple_of((lax.rem(z, 2) * 4 + x * 8) * D, WIDTH), WIDTH)


def pair_table(z, y, x, c, docs, mask, order):
    z_hi = lax.div(z, 2)
    row = lax.broadcasted_iota(jnp.int32, (T, T), 0)
    col = lax.broadcasted_iota(jnp.int32, (T, T), 1)
    doc_cols = jnp.broadcast_to(docs[...].astype(F32), (T, T))
    live = (mask[...] == 1) & (doc_cols.T == doc_cols) & (row >= col)
    live = jnp.where(live, 1.0, 0.0).astype(BF16)
    holds = jnp.where(row == jnp.broadcast_to(order[...], (T, T)), 1.0, 0.0).astype(BF16)
    by_key = jnp.dot(live, holds, preferred_element_type=F32).astype(BF16)
    stored = lax.dot_general(holds, by_key, TN, preferred_element_type=F32).astype(BF16)
    small_row = lax.broadcasted_iota(jnp.int32, (QUERY_TILES, T), 0)
    small_col = lax.broadcasted_iota(jnp.int32, (QUERY_TILES, T), 1)
    first = (z_hi * 4 + y) * QUERY_TILES
    pick = jnp.where(small_col == small_row + first, 1.0, 0.0).astype(BF16)
    mine = jnp.dot(pick, stored, preferred_element_type=F32).astype(BF16)
    slot_z, slot_y, slot_x = col // 16, col // 4 % 4, col % 4
    source = (slot_z // 2) * 64 + slot_y * 16 + c * 8 + slot_z % 2 * 4 + slot_x
    spread = jnp.where((row == source) & (col < KEY_TILES), 1.0, 0.0).astype(BF16)
    pairs = jnp.dot(mine, spread, preferred_element_type=F32)
    own = ((z_hi * 2 + small_row % 8 // 4) * 4 + y) * 4 + small_row % 4
    is_own = (small_col == own) & (small_row // 8 == c)
    diag = jnp.sum(jnp.where(is_own, pairs, 0.0), axis=1, keepdims=True)
    rest = jnp.where(is_own, 0.0, pairs)
    upto = jnp.where(row <= col, 1.0, 0.0).astype(BF16)
    rank = jnp.dot(rest.astype(BF16), upto, preferred_element_type=F32)
    count = jnp.sum(rest, axis=1, keepdims=True)
    numbers = lax.broadcasted_iota(jnp.int32, (8, T), 1).astype(F32).astype(BF16)
    lists = []
    for i in range(QUERY_TILES):
        at = jnp.where(rest[i : i + 1, :] > 0.5, rank[i : i + 1, :] - 1.0, -1.0)
        chosen = jnp.where(jnp.broadcast_to(at, (T, T)) == row.astype(F32), 1.0, 0.0).astype(BF16)
        lists.append(lax.dot_general(numbers, chosen, NT, preferred_element_type=F32)[:1])
    table = jnp.concatenate(lists, axis=0)
    table = jnp.where(small_col == KEY_TILES, count, table)
    table = jnp.where(small_col == KEY_TILES + 1, diag, table)
    table = table.astype(jnp.int32)
    return jnp.where(small_col == KEY_TILES + 2, jnp.where(small_row // 8 == c, own, 0), table)


def gather(
    queries, grad_out, keys, values, attn_in, logs_in, docs_in, mask_in, order_in,
    sibling_rows, kg, vg, stats, table_out,
    table, attn_out, log_sums, docs, mask, order,
    own_grad, stat_parts, sends, recvs, local,
):
    z, y, x, c = place()
    ka = lax.rem(z, 2) * 4 + x
    columns = head_columns(z, x)
    own_rows = pl.ds(pl.multiple_of(ka * T, T), T)
    loads = [
        pltpu.make_async_copy(source, target, local.at[6 + n])
        for n, (source, target) in enumerate(
            (
                (attn_in, attn_out),
                (logs_in, log_sums),
                (docs_in, docs),
                (mask_in, mask),
                (order_in, order),
            )
        )
    ]
    loads.append(pltpu.make_async_copy(grad_out.at[own_rows], own_grad, local.at[0]))
    for copy in loads:
        copy.start()

    def part(ref, to):
        return ref.at[:, pl.ds(pl.multiple_of(to * D, D), D)]

    peers = group_peers(z, y, x, c)
    y_plus, y_minus = ident(z, wrap(y + 1), x, c), ident(z, wrap(y - 1), x, c)
    z_plus, z_minus = ident(wrap(z + 1), y, x, c), ident(wrap(z - 1), y, x, c)
    far = ident(wrap(z + 2 * lax.rem(z, 2) - 1), y, x, c)
    greet([peer for _, _, peer in peers] + [y_plus, y_minus, far])

    slot = pl.ds(pl.multiple_of(x * T, T), T)
    across = Lane(sends, recvs, 0)
    for step in range(1, RING):
        to = wrap(x + step)
        across.send(part(keys, to), kg.at[z, y, slot], step - 1, ident(z, y, to, c))
        across.send(part(values, to), vg.at[z, y, slot], step + 2, ident(z, y, to, c))
    kept = [
        pltpu.make_async_copy(part(keys, x), kg.at[z, y, slot], local.at[3]),
        pltpu.make_async_copy(part(values, x), vg.at[z, y, slot], local.at[4]),
    ]
    for copy in kept:
        copy.start()
    sibling = ident(z, y, x, 1 - c)
    pair = Lane(sends, recvs, 6)
    pair.send(queries.at[:, columns], sibling_rows.at[0], 0, sibling)
    pair.send(grad_out.at[:, columns], sibling_rows.at[1], 1, sibling)

    for copy in kept:
        copy.wait()
    for step in range(1, RING):
        origin = wrap(x - step)
        came = pl.ds(pl.multiple_of(origin * T, T), T)
        across.arrive(kg.at[z, y, came], step - 1, ident(z, y, origin, c))
        across.arrive(vg.at[z, y, came], step + 2, ident(z, y, origin, c))

    def block(ref, dz, dy):
        return ref.at[wrap(z + dz), wrap(y + dy)]

    base = 24
    key_first = Spread(sends, recvs, base).setup(lambda o: block(kg, o, 0), z_plus, z_minus)
    value_first = Spread(sends, recvs, base + 4).setup(lambda o: block(vg, 0, o), y_plus, y_minus)
    key_then, value_then = {}, {}
    for n, off in enumerate((0, -1, 1, 2)):
        key_then[off] = Spread(sends, recvs, base + 8 + 4 * n).setup(
            lambda o, off=off: block(kg, off, o), y_plus, y_minus
        )
        value_then[off] = Spread(sends, recvs, base + 24 + 4 * n).setup(
            lambda o, off=off: block(vg, o, off), z_plus, z_minus
        )
    key_first.start()
    value_first.start()
    key_then[0].start()
    value_then[0].start()

    for copy in loads:
        copy.wait()
    for to in range(KA):
        first = to % 4 * 8 + to // 4 * 4
        stat_parts[to, 0:HEADS, :] = log_sums[first : first + HEADS, :]
        for h in range(HEADS):
            lanes = pl.ds((first + h) * D, D)
            product = own_grad[:, lanes].astype(F32) * attn_out[:, lanes].astype(F32)
            stat_parts[to, HEADS + h : HEADS + h + 1, :] = jnp.sum(product.T, axis=0, keepdims=True)
    share = Lane(sends, recvs, 8)
    for flip, step, peer in peers:
        share.send(stat_parts.at[lax.rem(ka + step, KA)], stats.at[c * KA + ka], flip * KA + step, peer)
    keep_stats = pltpu.make_async_copy(stat_parts.at[ka], stats.at[c * KA + ka], local.at[5])
    keep_stats.start()

    key_first.relay_up()
    value_first.relay_up()
    key_then[-1].start()
    value_then[-1].start()
    key_first.relay_down()
    value_first.relay_down()
    key_then[1].start()
    value_then[1].start()
    table[...] = pair_table(z, y, x, c, docs, mask, order)
    keep_table = pltpu.make_async_copy(table, table_out, local.at[11])
    keep_table.start()
    for off in (0,):
        key_then[off].relay_up()
        value_then[off].relay_up()
        key_then[off].relay_down()
        value_then[off].relay_down()
    key_first.finish()
    value_first.finish()
    key_then[2].start()
    value_then[2].start()
    for off in (-1, 1, 2):
        key_then[off].relay_up()
        value_then[off].relay_up()
        key_then[off].relay_down()
        value_then[off].relay_down()
    for off in (0, -1, 1, 2):
        key_then[off].finish()
        value_then[off].finish()

    pair.arrive(sibling_rows.at[0], 0, sibling)
    pair.arrive(sibling_rows.at[1], 1, sibling)
    for flip, step, _ in peers:
        origin = lax.rem(ka + KA - step, KA)
        core = 1 - c if flip else c
        from_ = ident(lax.div(z, 2) * 2 + lax.div(origin, 4), y, lax.rem(origin, 4), core)
        share.arrive(stats.at[core * KA + origin], flip * KA + step, from_)
    keep_stats.wait()
    keep_table.wait()
    for lane in [across, pair, share, key_first, value_first, *key_then.values(), *value_then.values()]:
        lane.drain()


def attend(
    table, stats_in, queries, grad_out, sibling_rows, keys_in, values_in, key_gain, value_gain,
    dq_ref, dk_ref, dv_ref, gains,
    plan, stats, q_ref, g_ref, keys, values, k_ref, v_ref, dk_acc, dv_acc, dq_acc, held, gain_acc, local,
):
    scale = D ** -0.5
    z, _, x, c = place()
    columns = head_columns(z, x)
    own, other = [pl.ds(pl.multiple_of(core * KA * T, KA * T), KA * T) for core in (c, 1 - c)]
    loads = [
        pltpu.make_async_copy(source, target, local.at[n])
        for n, (source, target) in enumerate(
            (
                (keys_in, keys),
                (values_in, values),
                (stats_in, stats),
                (queries.at[:, columns], q_ref.at[own]),
                (grad_out.at[:, columns], g_ref.at[own]),
                (sibling_rows.at[0], q_ref.at[other]),
                (sibling_rows.at[1], g_ref.at[other]),
            )
        )
    ]
    for copy in loads:
        copy.start()
    dk_acc[...] = jnp.zeros_like(dk_acc)
    dv_acc[...] = jnp.zeros_like(dv_acc)
    dq_acc[...] = jnp.zeros_like(dq_acc)

    def stack(ref, i):
        rows = pl.ds(pl.multiple_of(i * T, T), T)
        return jnp.concatenate([ref[rows, h * D : (h + 1) * D] for h in range(HEADS)], axis=0)

    def tiles(ref, a, b):
        parts = [ref[pl.ds(pl.multiple_of(at * T, T), T), :] for at in (a, b)]
        return jnp.concatenate(parts, axis=0)

    def unpack(step):
        word = plan[step]
        return word >> 16, (word >> 8) & 63, word & 63, (word >> 14) & 1, (word >> 6) & 1

    def front(step, slot, masked):
        i, a, b, use_a, use_b = unpack(step)
        s = lax.dot_general(tiles(k_ref, a, b), stack(q_ref, i), NT, preferred_element_type=F32)
        dp = lax.dot_general(tiles(v_ref, a, b), stack(g_ref, i), NT, preferred_element_type=F32)
        lse = jnp.concatenate([stats[i, h : h + 1, :] for h in range(HEADS)], axis=1) * LOG2E
        delta = jnp.concatenate([stats[i, HEADS + h : HEADS + h + 1, :] for h in range(HEADS)], axis=1)
        p = jnp.exp2(s * (scale * LOG2E) - lse)
        if masked:
            row = lax.broadcasted_iota(jnp.int32, (T, T), 0)
            col = lax.broadcasted_iota(jnp.int32, (T, T), 1)
            ok_a = row < use_a * T
            ok_b = row <= col - (1 - use_b) * T
            ok = jnp.concatenate(
                [jnp.concatenate([ok_a] * HEADS, axis=1), jnp.concatenate([ok_b] * HEADS, axis=1)], axis=0
            )
            p = jnp.where(ok, p, 0.0)
        held[slot, 0] = p.astype(BF16)
        held[slot, 1] = (p * (dp - delta)).astype(BF16)

    def back(step, slot):
        i, a, b, _, _ = unpack(step)
        p, ds = held[slot, 0], held[slot, 1]
        dv = jnp.dot(p, stack(g_ref, i), preferred_element_type=F32)
        dk = jnp.dot(ds, stack(q_ref, i), preferred_element_type=F32)
        dq_acc[i] += lax.dot_general(tiles(k_ref, a, b), ds, TN, preferred_element_type=F32)
        for n, at in enumerate((a, b)):
            rows = pl.ds(pl.multiple_of(at * T, T), T)
            dv_acc[rows, :] += dv[n * T : (n + 1) * T]
            dk_acc[rows, :] += dk[n * T : (n + 1) * T]

    def run(steps, masked, unroll):
        plan[steps] = 0
        front(0, 0, masked)

        def twos(first, count):
            for r in range(0, count, 2):
                front(first + r + 1, 1, masked)
                back(first + r, 0)
                front(first + r + 2, 0, masked)
                back(first + r + 1, 1)

        whole = lax.div(steps, unroll)

        @pl.loop(0, whole)
        def _(u):
            twos(u * unroll, unroll)

        if unroll > 2:

            @pl.loop(whole * (unroll // 2), lax.div(steps, 2))
            def _(u):
                twos(2 * u, 2)

        @pl.when(lax.rem(steps, 2) > 0)
        def _():
            back(steps - 1, 0)

    def list_whole(i, n):
        halves = lax.div(table[i, KEY_TILES], 2)

        def put(r, n):
            plan[n] = (i << 16) | (table[i, 2 * r] << 8) | table[i, 2 * r + 1]
            return n + 1

        return lax.fori_loop(0, halves, put, n)

    steps = lax.fori_loop(0, QUERY_TILES, list_whole, jnp.int32(0))
    lanes = pl.ds(pl.multiple_of(x * D, D), D)
    for n, (raw, scaled, gain) in enumerate(((keys, k_ref, key_gain), (values, v_ref, value_gain))):
        loads[n].wait()
        factor = gain[:, lanes]

        @pl.loop(0, KEY_TILES // 2)
        def _(n):
            at = pl.ds(pl.multiple_of(n * 2 * T, 2 * T), 2 * T)
            scaled[at, :] = (raw[at, :].astype(F32) * factor).astype(BF16)

    for copy in loads[2:]:
        copy.wait()
    run(steps, False, 8)

    def list_masked(i, n):
        count, diag = table[i, KEY_TILES], table[i, KEY_TILES + 1]
        odd = lax.rem(count, 2)
        last = table[i, jnp.maximum(count - 1, 0)]

        @pl.when(odd + diag > 0)
        def _():
            plan[n] = (i << 16) | (odd << 14) | (last << 8) | (diag << 6) | table[i, KEY_TILES + 2]

        return n + jnp.minimum(odd + diag, 1)

    run(lax.fori_loop(0, QUERY_TILES, list_masked, jnp.int32(0)), True, 4)

    @pl.loop(0, QUERY_TILES)
    def _(i):
        rows = pl.ds(pl.multiple_of(i * T, T), T)
        for h in range(HEADS):
            lanes = slice(h * D, (h + 1) * D)
            dq_ref[rows, lanes] = (dq_acc[i, :, lanes] * scale).astype(BF16).T

    gain_acc[...] = jnp.zeros_like(gain_acc)

    @pl.loop(0, KEY_TILES)
    def _(n):
        at = pl.ds(pl.multiple_of(n * T, T), T)
        dkey, dvalue = dk_acc[at, :] * scale, dv_acc[at, :]
        owner = (lax.div(n, 16), lax.rem(lax.div(n, 4), 4), lax.rem(n, 4))
        dk_ref[owner] = dkey.astype(BF16)
        dv_ref[owner] = dvalue.astype(BF16)
        gain_acc[0] += jnp.sum((dkey * keys[at, :].astype(F32)).reshape(T // 8, 8, D), axis=0)
        gain_acc[1] += jnp.sum((dvalue * values[at, :].astype(F32)).reshape(T // 8, 8, D), axis=0)

    gains[...] = jnp.zeros_like(gains)
    for n in range(2):
        gains[n : n + 1, :] = jnp.sum(gain_acc[n], axis=0, keepdims=True)


def scatter(
    dq, dk, dv, partial, key_gain, value_gain,
    grad_queries, grad_keys, grad_values, grad_key_gain, grad_value_gain,
    dq_in, land_z, land_v, land_k, out_k, out_v, in_k, in_v, near, total, sends, recvs,
):
    z, y, x, c = place()
    ka = lax.rem(z, 2) * 4 + x
    z_hi, z_lo = lax.div(z, 2), lax.rem(z, 2)
    y_plus, y_minus = ident(z, wrap(y + 1), x, c), ident(z, wrap(y - 1), x, c)
    z_far, z_near = ident(wrap(z + 2 * z_lo - 1), y, x, c), ident(wrap(z + 1 - 2 * z_lo), y, x, c)
    steps = [(one, two) for one in range(RING) for two in range(RING) if one or two]
    in_y = [ident(z, wrap(y + one), wrap(x + two), c) for one, two in steps]
    in_z = [ident(wrap(z + one), y, wrap(x + two), c) for one, two in steps]
    others = [(0, one, ident(wrap(z + one), y, x, c)) for one in range(1, RING)]
    others += [(1, one, ident(wrap(z + one), y, x, 1 - c)) for one in range(RING)]
    greet(in_y + [peer for peer, (one, _) in zip(in_z, steps) if one] + [other for flip, _, other in others if flip])

    spread = Lane(sends, recvs, 56)
    for (one, two), peer in zip(steps, in_y):
        spread.send(partial, near.at[one, two], one * RING + two, peer)
    near[0, 0] = partial[...]

    sibling = ident(z, y, x, 1 - c)
    pair = Lane(sends, recvs, 0)
    for n in range(KA):
        to = lax.rem(ka + n + 1, KA)
        rows = pl.ds(pl.multiple_of(((1 - c) * KA + to) * T, T), T)
        pair.send(dq.at[rows], dq_in.at[to], n, sibling)

    keys_z = Detour(sends, recvs, 16).setup(
        lambda at: dk.at[at, :, pl.ds(0, Z_FIRST)], [pl.ds(0, 2), pl.ds(2, 2)], land_z, z, z_far, z_near
    )
    last_y = Fold(sends, recvs, 22).setup(
        lambda off, n: dk.at[pl.ds(2 * n, 2), wrap(y + off), pl.ds(Z_FIRST, RING - Z_FIRST)], land_k, y_plus, y_minus
    )
    rows_of = [pl.ds(n * (T // PARTS), T // PARTS) for n in range(PARTS)]
    values_y = [
        Fold(sends, recvs, 72 + 22 * part).setup(
            lambda off, n, rows=rows: dv.at[pl.ds(2 * n, 2), wrap(y + off), :, rows], land_v.at[part], y_plus, y_minus
        )
        for part, rows in enumerate(rows_of)
    ]
    keys_z.start()
    last_y.start()
    for lane in values_y:
        lane.start()

    lane_q = Lane(sends, recvs, 8)
    columns = head_columns(z, x)
    for n in range(KA):
        to = lax.rem(ka + n + 1, KA)
        own_rows = dq.at[pl.ds(pl.multiple_of((c * KA + to) * T, T), T)]
        pair.arrive(dq_in.at[to], n, sibling)
        for h in range(HEADS):
            lanes = pl.ds(h * D, D)
            value = own_rows[:, lanes].astype(F32) + dq_in[to, :, lanes].astype(F32)
            dq_in[to, :, lanes] = value.astype(BF16)
        if n < KA - 1:
            peer = ident(z_hi * 2 + lax.div(to, 4), y, lax.rem(to, 4), c)
            lane_q.send(dq_in.at[to], grad_queries.at[:, columns], n + 1, peer)
    grad_queries[:, columns] = dq_in[ka]

    for (one, two), peer in zip(steps, in_y):
        spread.arrive(near.at[one, two], one * RING + two, peer)
    for n in range(RING):
        block = near[wrap(y), wrap(x - n + RING)]
        for one in range(1, RING):
            block = block + near[wrap(y - one + RING), wrap(x - n + RING)]
        total[0, 2 * n : 2 * n + 2, :] = block[0:2]
    mine = c * RING + z
    total[1 + mine] = total[0]
    share = Lane(sends, recvs, 28)
    for flip, step, other in others:
        share.send(total.at[0], total.at[1 + mine], flip * RING + step, other)

    def finish_values(part):
        values_y[part].finish([out_v.at[pl.ds(2 * n, 2), :, rows_of[part]] for n in range(2)])

    last_y.relay()
    keys_z.relay(0)
    values_y[0].relay()
    keys_z.relay(1)
    last_y.finish([out_k.at[pl.ds(2 * n, 2), pl.ds(Z_FIRST, RING - Z_FIRST)] for n in range(2)])
    finish_values(0)

    def send_values(part):
        lane = Lane(sends, recvs, 78 + 22 * part)
        for (one, two), peer in zip(steps, in_z):
            block = out_v.at[wrap(z + one), wrap(x + two), rows_of[part]]
            lane.send(block, in_v.at[one, two, rows_of[part]], one * RING + two, peer)
        return lane

    values_out = [send_values(0)]
    for part in range(1, PARTS):
        values_y[part].relay()
        finish_values(part)
        values_out.append(send_values(part))
    keys_z.finish(out_k.at[:, pl.ds(0, Z_FIRST)])
    keys_out = Lane(sends, recvs, 40)
    for one, two in steps:
        to = wrap(x + two)
        over_z = lax.div(to, Z_FIRST)
        to_z, to_y = wrap(z + one * over_z), wrap(y + one * (1 - over_z))
        block = out_k.at[over_z * to_z + (1 - over_z) * to_y, to]
        keys_out.send(block, in_k.at[one, two], one * RING + two, ident(to_z, to_y, to, c))

    def deliver(result, gain, own, came):
        for two in range(RING):
            lanes = pl.ds(pl.multiple_of(wrap(x - two) * D, D), D)
            value = (own if two == 0 else came[0, two]).astype(F32)
            for one in range(1, RING):
                value = value + came[one, two].astype(F32)
            result[:, lanes] = (value * gain[:, lanes]).astype(BF16)

    for (one, two), peer in zip(steps, in_y):
        keys_out.arrive(in_k.at[one, two], one * RING + two, peer)
    own_over_z = lax.div(x, Z_FIRST)
    deliver(grad_keys, key_gain, out_k[own_over_z * z + (1 - own_over_z) * y, x], in_k)
    for part in range(PARTS):
        for (one, two), peer in zip(steps, in_z):
            values_out[part].arrive(in_v.at[one, two, rows_of[part]], one * RING + two, peer)
    deliver(grad_values, value_gain, out_v[z, x], in_v)

    for flip, step, other in others:
        origin = (1 - c if flip else c) * RING + wrap(z - step)
        share.arrive(total.at[1 + origin], flip * RING + step, other)
    whole = jnp.sum(total[1:], axis=0)
    for n in range(RING):
        grad_key_gain[:, n * D : (n + 1) * D] = whole[2 * n : 2 * n + 1]
        grad_value_gain[:, n * D : (n + 1) * D] = whole[2 * n + 1 : 2 * n + 2]
    for n in range(1, KA):
        origin = lax.rem(ka + KA - n, KA)
        their = head_columns(lax.div(origin, 4), lax.rem(origin, 4))
        from_ = ident(z_hi * 2 + lax.div(origin, 4), y, lax.rem(origin, 4), c)
        lane_q.arrive(grad_queries.at[:, their], n, from_)
    for lane in [
        pair, lane_q, keys_z, last_y, *values_y, keys_out, *values_out, share, spread
    ]:
        lane.drain()


def shape(dims, dtype):
    return jax.ShapeDtypeStruct(dims, dtype)


def attend_call(table, stats, queries, grad_out, sibling_rows, k, v, key_gain, value_gain):
    vm, hbm = pl.BlockSpec(memory_space=pltpu.VMEM), pl.BlockSpec(memory_space=pl.ANY)
    return pl.pallas_call(
        attend,
        out_shape=(shape((2 * KA * T, WIDTH), BF16), *[shape((RING, RING, RING, T, D), BF16)] * 2, shape((8, D), F32)),
        in_specs=[pl.BlockSpec(memory_space=pltpu.SMEM)] + [hbm] * 6 + [vm] * 2,
        out_specs=(vm,) * 4,
        scratch_shapes=[
            pltpu.SMEM((QUERY_TILES * KEY_TILES // 2 + 2,), jnp.int32),
            pltpu.VMEM(stats.shape, F32),
            pltpu.VMEM((2 * KA * T, WIDTH), BF16),
            pltpu.VMEM((2 * KA * T, WIDTH), BF16),
            pltpu.VMEM(k.shape, BF16),
            pltpu.VMEM(v.shape, BF16),
            pltpu.VMEM(k.shape, BF16),
            pltpu.VMEM(v.shape, BF16),
            pltpu.VMEM(k.shape, F32),
            pltpu.VMEM(v.shape, F32),
            pltpu.VMEM((QUERY_TILES, D, WIDTH), F32),
            pltpu.VMEM((2, 2, 2 * T, WIDTH), BF16),
            pltpu.VMEM((2, 8, D), F32),
            pltpu.SemaphoreType.DMA((7,)),
        ],
        compiler_params=pltpu.CompilerParams(vmem_limit_bytes=47 * 2**20),
        name="attend",
    )(table, stats, queries, grad_out, sibling_rows, k, v, key_gain, value_gain)


def shards(
    queries, key_rows, values, attn_out, grad_out, log_sums, key_gain, value_gain, doc_ids, tile_mask, block_order
):
    vm, hbm = pl.BlockSpec(memory_space=pltpu.VMEM), pl.BlockSpec(memory_space=pl.ANY)
    key_gain, value_gain = key_gain.reshape(1, -1), value_gain.reshape(1, -1)
    rows = queries.shape[0]
    sibling_rows, kg, vg, stats, table = pl.pallas_call(
        gather,
        out_shape=(
            shape((2, rows, WIDTH), BF16),
            shape((RING, RING, RING * T, D), BF16),
            shape((RING, RING, RING * T, D), BF16),
            shape((QUERY_TILES, 2 * HEADS, T), F32),
            shape((QUERY_TILES, T), jnp.int32),
        ),
        in_specs=[hbm] * 9,
        out_specs=(hbm,) * 5,
        scratch_shapes=[
            pltpu.VMEM((QUERY_TILES, T), jnp.int32),
            pltpu.VMEM(attn_out.shape, BF16),
            pltpu.VMEM(log_sums.shape, F32),
            pltpu.VMEM((1, T), jnp.int32),
            pltpu.VMEM(tile_mask.shape, jnp.int32),
            pltpu.VMEM((1, T), jnp.int32),
            pltpu.VMEM(attn_out.shape, BF16),
            pltpu.VMEM((KA, 2 * HEADS, T), F32),
            pltpu.SemaphoreType.DMA((64,)),
            pltpu.SemaphoreType.DMA((64,)),
            pltpu.SemaphoreType.DMA((12,)),
        ],
        compiler_params=pltpu.CompilerParams(
            collective_id=0, has_side_effects=True, vmem_limit_bytes=56 * 2**20
        ),
        name="gather",
    )(
        queries, grad_out, key_rows, values, attn_out, log_sums,
        doc_ids.reshape(1, -1), tile_mask, block_order.reshape(1, -1),
    )
    dq, dk, dv, partial = attend_call(
        table, stats, queries, grad_out, sibling_rows,
        kg.reshape(KEY_TILES * T, D), vg.reshape(KEY_TILES * T, D), key_gain, value_gain,
    )
    grad_queries, grad_keys, grad_values, grad_key_gain, grad_value_gain = pl.pallas_call(
        scatter,
        out_shape=(
            shape(attn_out.shape, BF16),
            shape(key_rows.shape, BF16),
            shape(values.shape, BF16),
            shape(key_gain.shape, F32),
            shape(value_gain.shape, F32),
        ),
        in_specs=[vm] * 6,
        out_specs=(vm,) * 5,
        scratch_shapes=[
            pltpu.VMEM((KA, T, WIDTH), BF16),
            pltpu.VMEM((3, RING, Z_FIRST, T, D), BF16),
            pltpu.VMEM((PARTS, 6, 2, RING, T // PARTS, D), BF16),
            pltpu.VMEM((6, 2, RING - Z_FIRST, T, D), BF16),
            pltpu.VMEM((RING, RING, T, D), BF16),
            pltpu.VMEM((RING, RING, T, D), BF16),
            pltpu.VMEM((RING, RING, T, D), BF16),
            pltpu.VMEM((RING, RING, T, D), BF16),
            pltpu.VMEM((RING, RING, 8, D), F32),
            pltpu.VMEM((9, 8, D), F32),
            pltpu.SemaphoreType.DMA((72 + 22 * PARTS,)),
            pltpu.SemaphoreType.DMA((72 + 22 * PARTS,)),
        ],
        compiler_params=pltpu.CompilerParams(
            collective_id=1, has_side_effects=True, vmem_limit_bytes=20 * 2**20
        ),
        name="scatter",
    )(dq, dk, dv, partial, key_gain, value_gain)
    return grad_queries, grad_keys, grad_values, grad_key_gain.reshape(-1), grad_value_gain.reshape(-1)


def solution(mesh):
    rows = P(("pb", "ka"), None)
    placed = (P("pb", None), rows, rows, rows, P("pb", None), P(None, ("pb", "ka")), P(), P(), P(), P(), P())
    return jax.shard_map(
        shards, mesh=mesh, in_specs=placed, out_specs=(rows, rows, rows, P(), P()), check_vma=False
    )
```

```python
import functools
import math

import jax
import jax.numpy as jnp
from jax import lax
from jax.experimental import pallas as pl
from jax.experimental.pallas import tpu as pltpu
from jax.sharding import PartitionSpec as P


D = 128
T = 128
RING = 4
KA = 8
HEADS = 4
WIDTH = HEADS * D
QUERY_TILES = 16
KEY_TILES = 64
Z_FIRST = 3
PARTS = 2
LOG2E = math.log2(math.e)
MESH = pl.DeviceIdType.MESH
F32 = jnp.float32
BF16 = jnp.bfloat16
NT = (((1,), (1,)), ((), ()))
TN = (((0,), (0,)), ((), ()))


def wrap(at):
    return lax.rem(at + RING, RING)


def place():
    pb, ka = lax.axis_index("pb"), lax.axis_index("ka")
    z = lax.div(pb, 8) * 2 + lax.div(ka, 4)
    return z, lax.rem(lax.div(pb, 2), 4), lax.rem(ka, 4), lax.rem(pb, 2)


def ident(z, y, x, c):
    return (lax.div(z, 2) * 8 + y * 2 + c, lax.rem(z, 2) * 4 + x)


def group_peers(z, y, x, c):
    ka = lax.rem(z, 2) * 4 + x
    peers = []
    for flip in range(2):
        for step in range(KA):
            if flip or step:
                to = lax.rem(ka + step, KA)
                core = 1 - c if flip else c
                peers.append((flip, step, ident(lax.div(z, 2) * 2 + lax.div(to, 4), y, lax.rem(to, 4), core)))
    return peers


def greet(devices):
    barrier = pltpu.get_barrier_semaphore()
    for device in devices:
        pl.semaphore_signal(barrier, inc=1, device_id=device, device_id_type=MESH)
    pl.semaphore_wait(barrier, len(devices))


class Lane:
    def __init__(self, sends, recvs, base):
        self.sends, self.recvs, self.base, self.out = sends, recvs, base, []

    def send(self, source, target, number, device):
        copy = pltpu.make_async_remote_copy(
            src_ref=source,
            dst_ref=target,
            send_sem=self.sends.at[self.base + number],
            recv_sem=self.recvs.at[self.base + number],
            device_id=device,
            device_id_type=MESH,
        )
        copy.start()
        self.out.append(copy)

    def arrive(self, target, number, device):
        pltpu.make_async_remote_copy(
            src_ref=target,
            dst_ref=target,
            send_sem=self.sends.at[self.base + number],
            recv_sem=self.recvs.at[self.base + number],
            device_id=device,
            device_id_type=MESH,
        ).wait_recv()

    def drain(self):
        for copy in self.out:
            copy.wait_send()
        self.out = []


class Spread(Lane):
    def setup(self, item, plus, minus):
        self.item, self.plus, self.minus = item, plus, minus
        half = item(0).shape[0] // 2
        self.first, self.second = pl.ds(0, half), pl.ds(half, half)
        return self

    def start(self):
        self.send(self.item(0), self.item(0), 0, self.plus)
        self.send(self.item(0), self.item(0), 1, self.minus)

    def relay_up(self):
        block = self.item(-1)
        self.arrive(block, 0, self.minus)
        self.send(block.at[self.first], block.at[self.first], 2, self.plus)

    def relay_down(self):
        block = self.item(1)
        self.arrive(block, 1, self.plus)
        self.send(block.at[self.second], block.at[self.second], 3, self.minus)

    def finish(self):
        block = self.item(2)
        self.arrive(block.at[self.first], 2, self.minus)
        self.arrive(block.at[self.second], 3, self.plus)


class Fold(Lane):
    def setup(self, half_of, land, plus, minus):
        self.half_of, self.land, self.plus, self.minus = half_of, land, plus, minus
        return self

    def start(self):
        self.send(self.half_of(2, 0), self.land.at[0], 0, self.plus)
        self.send(self.half_of(2, 1), self.land.at[1], 1, self.minus)
        self.send(self.half_of(1, 1), self.land.at[3], 3, self.plus)
        self.send(self.half_of(-1, 0), self.land.at[4], 4, self.minus)

    def relay(self):
        self.arrive(self.land.at[0], 0, self.minus)
        combine(self.land.at[0], [self.land.at[0], self.half_of(1, 0)])
        self.send(self.land.at[0], self.land.at[2], 2, self.plus)
        self.arrive(self.land.at[1], 1, self.plus)
        combine(self.land.at[1], [self.land.at[1], self.half_of(-1, 1)])
        self.send(self.land.at[1], self.land.at[5], 5, self.minus)

    def finish(self, totals):
        self.arrive(self.land.at[3], 3, self.minus)
        self.arrive(self.land.at[4], 4, self.plus)
        self.arrive(self.land.at[2], 2, self.minus)
        combine(totals[0], [self.half_of(0, 0), self.land.at[2], self.land.at[4]])
        self.arrive(self.land.at[5], 5, self.plus)
        combine(totals[1], [self.half_of(0, 1), self.land.at[3], self.land.at[5]])


class Detour(Lane):
    def setup(self, item, cuts, land, z, hi, lo):
        self.item, self.cuts, self.land, self.z, self.hi, self.lo = item, cuts, land, z, hi, lo
        side = 2 * lax.rem(z, 2) - 1
        self.at_hi, self.at_lo, self.at_far = wrap(z + side), wrap(z - side), wrap(z + 2)
        return self

    def start(self):
        for n, cut in enumerate(self.cuts):
            self.send(self.item(self.at_far).at[cut], self.land.at[0].at[cut], n, self.hi)
        self.send(self.item(self.at_hi), self.land.at[1], len(self.cuts), self.hi)

    def relay(self, n):
        cut = self.cuts[n]
        passed = self.land.at[0].at[cut]
        self.arrive(passed, n, self.hi)
        combine(passed, [passed, self.item(self.at_lo).at[cut]])
        self.send(passed, self.land.at[2].at[cut], len(self.cuts) + 1 + n, self.lo)

    def finish(self, total):
        self.arrive(self.land.at[1], len(self.cuts), self.hi)
        for n, cut in enumerate(self.cuts):
            self.arrive(self.land.at[2].at[cut], len(self.cuts) + 1 + n, self.lo)
        combine(total, [self.item(self.z), self.land.at[1], self.land.at[2]])


def combine(total, terms):
    lead = total.shape[:-2]

    @pl.loop(0, math.prod(lead))
    def _(n):
        at = []
        for extent in reversed(lead):
            at.append(lax.rem(n, extent))
            n = lax.div(n, extent)
        at = tuple(reversed(at))
        value = terms[0][at].astype(F32)
        for term in terms[1:]:
            value = value + term[at].astype(F32)
        total[at] = value.astype(total.dtype)


def head_columns(z, x):
    return pl.ds(pl.multiple_of((lax.rem(z, 2) * 4 + x * 8) * D, WIDTH), WIDTH)


def pair_table(z, y, x, c, docs, mask, order):
    z_hi = lax.div(z, 2)
    row = lax.broadcasted_iota(jnp.int32, (T, T), 0)
    col = lax.broadcasted_iota(jnp.int32, (T, T), 1)
    doc_cols = jnp.broadcast_to(docs[...].astype(F32), (T, T))
    live = (mask[...] == 1) & (doc_cols.T == doc_cols) & (row >= col)
    live = jnp.where(live, 1.0, 0.0).astype(BF16)
    holds = jnp.where(row == jnp.broadcast_to(order[...], (T, T)), 1.0, 0.0).astype(BF16)
    by_key = jnp.dot(live, holds, preferred_element_type=F32).astype(BF16)
    stored = lax.dot_general(holds, by_key, TN, preferred_element_type=F32).astype(BF16)
    small_row = lax.broadcasted_iota(jnp.int32, (QUERY_TILES, T), 0)
    small_col = lax.broadcasted_iota(jnp.int32, (QUERY_TILES, T), 1)
    first = (z_hi * 4 + y) * QUERY_TILES
    pick = jnp.where(small_col == small_row + first, 1.0, 0.0).astype(BF16)
    mine = jnp.dot(pick, stored, preferred_element_type=F32).astype(BF16)
    slot_z, slot_y, slot_x = col // 16, col // 4 % 4, col % 4
    source = (slot_z // 2) * 64 + slot_y * 16 + c * 8 + slot_z % 2 * 4 + slot_x
    spread = jnp.where((row == source) & (col < KEY_TILES), 1.0, 0.0).astype(BF16)
    pairs = jnp.dot(mine, spread, preferred_element_type=F32)
    own = ((z_hi * 2 + small_row % 8 // 4) * 4 + y) * 4 + small_row % 4
    is_own = (small_col == own) & (small_row // 8 == c)
    diag = jnp.sum(jnp.where(is_own, pairs, 0.0), axis=1, keepdims=True)
    rest = jnp.where(is_own, 0.0, pairs)
    upto = jnp.where(row <= col, 1.0, 0.0).astype(BF16)
    rank = jnp.dot(rest.astype(BF16), upto, preferred_element_type=F32)
    count = jnp.sum(rest, axis=1, keepdims=True)
    numbers = lax.broadcasted_iota(jnp.int32, (8, T), 1).astype(F32).astype(BF16)
    lists = []
    for i in range(QUERY_TILES):
        at = jnp.where(rest[i : i + 1, :] > 0.5, rank[i : i + 1, :] - 1.0, -1.0)
        chosen = jnp.where(jnp.broadcast_to(at, (T, T)) == row.astype(F32), 1.0, 0.0).astype(BF16)
        lists.append(lax.dot_general(numbers, chosen, NT, preferred_element_type=F32)[:1])
    table = jnp.concatenate(lists, axis=0)
    table = jnp.where(small_col == KEY_TILES, count, table)
    table = jnp.where(small_col == KEY_TILES + 1, diag, table)
    table = table.astype(jnp.int32)
    return jnp.where(small_col == KEY_TILES + 2, jnp.where(small_row // 8 == c, own, 0), table)


def gather(
    queries, grad_out, keys, values, attn_in, logs_in, docs_in, mask_in, order_in,
    sibling_rows, kg, vg, stats, table_out,
    table, attn_out, log_sums, docs, mask, order,
    own_grad, stat_parts, sends, recvs, local,
):
    z, y, x, c = place()
    ka = lax.rem(z, 2) * 4 + x
    columns = head_columns(z, x)
    own_rows = pl.ds(pl.multiple_of(ka * T, T), T)
    loads = [
        pltpu.make_async_copy(source, target, local.at[6 + n])
        for n, (source, target) in enumerate(
            (
                (attn_in, attn_out),
                (logs_in, log_sums),
                (docs_in, docs),
                (mask_in, mask),
                (order_in, order),
            )
        )
    ]
    loads.append(pltpu.make_async_copy(grad_out.at[own_rows], own_grad, local.at[0]))
    for copy in loads:
        copy.start()

    def part(ref, to):
        return ref.at[:, pl.ds(pl.multiple_of(to * D, D), D)]

    peers = group_peers(z, y, x, c)
    y_plus, y_minus = ident(z, wrap(y + 1), x, c), ident(z, wrap(y - 1), x, c)
    z_plus, z_minus = ident(wrap(z + 1), y, x, c), ident(wrap(z - 1), y, x, c)
    far = ident(wrap(z + 2 * lax.rem(z, 2) - 1), y, x, c)
    greet([peer for _, _, peer in peers] + [y_plus, y_minus, far])

    slot = pl.ds(pl.multiple_of(x * T, T), T)
    across = Lane(sends, recvs, 0)
    for step in range(1, RING):
        to = wrap(x + step)
        across.send(part(keys, to), kg.at[z, y, slot], step - 1, ident(z, y, to, c))
        across.send(part(values, to), vg.at[z, y, slot], step + 2, ident(z, y, to, c))
    kept = [
        pltpu.make_async_copy(part(keys, x), kg.at[z, y, slot], local.at[3]),
        pltpu.make_async_copy(part(values, x), vg.at[z, y, slot], local.at[4]),
    ]
    for copy in kept:
        copy.start()
    sibling = ident(z, y, x, 1 - c)
    pair = Lane(sends, recvs, 6)
    pair.send(queries.at[:, columns], sibling_rows.at[0], 0, sibling)
    pair.send(grad_out.at[:, columns], sibling_rows.at[1], 1, sibling)

    for copy in kept:
        copy.wait()
    for step in range(1, RING):
        origin = wrap(x - step)
        came = pl.ds(pl.multiple_of(origin * T, T), T)
        across.arrive(kg.at[z, y, came], step - 1, ident(z, y, origin, c))
        across.arrive(vg.at[z, y, came], step + 2, ident(z, y, origin, c))

    def block(ref, dz, dy):
        return ref.at[wrap(z + dz), wrap(y + dy)]

    base = 24
    key_first = Spread(sends, recvs, base).setup(lambda o: block(kg, o, 0), z_plus, z_minus)
    value_first = Spread(sends, recvs, base + 4).setup(lambda o: block(vg, 0, o), y_plus, y_minus)
    key_then, value_then = {}, {}
    for n, off in enumerate((0, -1, 1, 2)):
        key_then[off] = Spread(sends, recvs, base + 8 + 4 * n).setup(
            lambda o, off=off: block(kg, off, o), y_plus, y_minus
        )
        value_then[off] = Spread(sends, recvs, base + 24 + 4 * n).setup(
            lambda o, off=off: block(vg, o, off), z_plus, z_minus
        )
    key_first.start()
    value_first.start()
    key_then[0].start()
    value_then[0].start()

    for copy in loads:
        copy.wait()
    for to in range(KA):
        first = to % 4 * 8 + to // 4 * 4
        stat_parts[to, 0:HEADS, :] = log_sums[first : first + HEADS, :]
        for h in range(HEADS):
            lanes = pl.ds((first + h) * D, D)
            product = own_grad[:, lanes].astype(F32) * attn_out[:, lanes].astype(F32)
            stat_parts[to, HEADS + h : HEADS + h + 1, :] = jnp.sum(product.T, axis=0, keepdims=True)
    share = Lane(sends, recvs, 8)
    for flip, step, peer in peers:
        share.send(stat_parts.at[lax.rem(ka + step, KA)], stats.at[c * KA + ka], flip * KA + step, peer)
    keep_stats = pltpu.make_async_copy(stat_parts.at[ka], stats.at[c * KA + ka], local.at[5])
    keep_stats.start()

    key_first.relay_up()
    value_first.relay_up()
    key_then[-1].start()
    value_then[-1].start()
    key_first.relay_down()
    value_first.relay_down()
    key_then[1].start()
    value_then[1].start()
    table[...] = pair_table(z, y, x, c, docs, mask, order)
    keep_table = pltpu.make_async_copy(table, table_out, local.at[11])
    keep_table.start()
    for off in (0,):
        key_then[off].relay_up()
        value_then[off].relay_up()
        key_then[off].relay_down()
        value_then[off].relay_down()
    key_first.finish()
    value_first.finish()
    key_then[2].start()
    value_then[2].start()
    for off in (-1, 1, 2):
        key_then[off].relay_up()
        value_then[off].relay_up()
        key_then[off].relay_down()
        value_then[off].relay_down()
    for off in (0, -1, 1, 2):
        key_then[off].finish()
        value_then[off].finish()

    pair.arrive(sibling_rows.at[0], 0, sibling)
    pair.arrive(sibling_rows.at[1], 1, sibling)
    for flip, step, _ in peers:
        origin = lax.rem(ka + KA - step, KA)
        core = 1 - c if flip else c
        from_ = ident(lax.div(z, 2) * 2 + lax.div(origin, 4), y, lax.rem(origin, 4), core)
        share.arrive(stats.at[core * KA + origin], flip * KA + step, from_)
    keep_stats.wait()
    keep_table.wait()
    for lane in [across, pair, share, key_first, value_first, *key_then.values(), *value_then.values()]:
        lane.drain()


def attend(
    table, stats_in, queries, grad_out, sibling_rows, keys_in, values_in, key_gain, value_gain,
    dq_ref, dk_ref, dv_ref, gains,
    plan, stats, q_ref, g_ref, keys, values, k_ref, v_ref, dk_acc, dv_acc, dq_acc, held, gain_acc, local,
):
    scale = D ** -0.5
    z, _, x, c = place()
    columns = head_columns(z, x)
    own, other = [pl.ds(pl.multiple_of(core * KA * T, KA * T), KA * T) for core in (c, 1 - c)]
    loads = [
        pltpu.make_async_copy(source, target, local.at[n])
        for n, (source, target) in enumerate(
            (
                (keys_in, keys),
                (values_in, values),
                (stats_in, stats),
                (queries.at[:, columns], q_ref.at[own]),
                (grad_out.at[:, columns], g_ref.at[own]),
                (sibling_rows.at[0], q_ref.at[other]),
                (sibling_rows.at[1], g_ref.at[other]),
            )
        )
    ]
    for copy in loads:
        copy.start()
    dk_acc[...] = jnp.zeros_like(dk_acc)
    dv_acc[...] = jnp.zeros_like(dv_acc)
    dq_acc[...] = jnp.zeros_like(dq_acc)

    def stack(ref, i):
        rows = pl.ds(pl.multiple_of(i * T, T), T)
        return jnp.concatenate([ref[rows, h * D : (h + 1) * D] for h in range(HEADS)], axis=0)

    def tiles(ref, places):
        parts = [ref[pl.ds(pl.multiple_of(at * T, T), T), :] for at in places]
        return parts[0] if len(parts) == 1 else jnp.concatenate(parts, axis=0)

    def unpack(step, width):
        word = plan[step]
        places = ((word >> 8) & 63, word & 63)
        return word >> 16, places[2 - width :], (word >> 6) & 1

    def front(step, slot, masked, width):
        i, places, diag = unpack(step, width)
        s = lax.dot_general(tiles(k_ref, places), stack(q_ref, i), NT, preferred_element_type=F32)
        dp = lax.dot_general(tiles(v_ref, places), stack(g_ref, i), NT, preferred_element_type=F32)
        lse = jnp.concatenate([stats[i, h : h + 1, :] for h in range(HEADS)], axis=1) * LOG2E
        delta = jnp.concatenate([stats[i, HEADS + h : HEADS + h + 1, :] for h in range(HEADS)], axis=1)
        p = jnp.exp2(s * (scale * LOG2E) - lse)
        if masked:
            row = lax.broadcasted_iota(jnp.int32, (T, T), 0)
            col = lax.broadcasted_iota(jnp.int32, (T, T), 1)
            ok = jnp.concatenate([row <= col + (1 - diag) * T] * HEADS, axis=1)
            last = jnp.where(ok, p[-T:], 0.0)
            p = last if width == 1 else jnp.concatenate([p[:T], last], axis=0)
        rows = slice(0, width * T)
        held[slot, 0, rows] = p.astype(BF16)
        held[slot, 1, rows] = (p * (dp - delta)).astype(BF16)

    def back(step, slot, width):
        i, places, _ = unpack(step, width)
        rows = slice(0, width * T)
        p, ds = held[slot, 0, rows], held[slot, 1, rows]
        dv = jnp.dot(p, stack(g_ref, i), preferred_element_type=F32)
        dk = jnp.dot(ds, stack(q_ref, i), preferred_element_type=F32)
        dq_acc[i] += lax.dot_general(tiles(k_ref, places), ds, TN, preferred_element_type=F32)
        for n, at in enumerate(places):
            rows = pl.ds(pl.multiple_of(at * T, T), T)
            dv_acc[rows, :] += dv[n * T : (n + 1) * T]
            dk_acc[rows, :] += dk[n * T : (n + 1) * T]

    def run(base, steps, masked, width, unroll):
        @pl.when(steps > 0)
        def _():
            plan[base + steps] = 0
            front(base, 0, masked, width)

        def twos(first, count):
            for r in range(0, count, 2):
                at = base + first + r
                front(at + 1, 1, masked, width)
                back(at, 0, width)
                front(at + 2, 0, masked, width)
                back(at + 1, 1, width)

        rounds = lax.div(steps, unroll)

        @pl.loop(0, rounds)
        def _(u):
            twos(u * unroll, unroll)

        if unroll > 2:

            @pl.loop(rounds * (unroll // 2), lax.div(steps, 2))
            def _(u):
                twos(2 * u, 2)

        @pl.when(lax.rem(steps, 2) > 0)
        def _():
            back(base + steps - 1, 0, width)

    base_both = QUERY_TILES * KEY_TILES // 2 + 1
    base_one = base_both + QUERY_TILES + 1

    def list_tile(i, counts):
        whole, both, one = counts
        count, diag = table[i, KEY_TILES], table[i, KEY_TILES + 1]

        def put(r, n):
            plan[n] = (i << 16) | (table[i, 2 * r] << 8) | table[i, 2 * r + 1]
            return n + 1

        whole = lax.fori_loop(0, lax.div(count, 2), put, whole)
        odd = lax.rem(count, 2)
        left = table[i, jnp.maximum(count - 1, 0)]
        own = table[i, KEY_TILES + 2]
        at = jnp.where(odd + diag == 2, base_both + both, base_one + one)
        plan[at] = (i << 16) | (left << 8) | (diag << 6) | (own * diag + left * (1 - diag))
        return whole, both + odd * diag, one + jnp.where(odd + diag == 1, 1, 0)

    zero = jnp.int32(0)
    whole, both, one = lax.fori_loop(0, QUERY_TILES, list_tile, (zero, zero, zero))
    lanes = pl.ds(pl.multiple_of(x * D, D), D)
    for n, (raw, scaled, gain) in enumerate(((keys, k_ref, key_gain), (values, v_ref, value_gain))):
        loads[n].wait()
        factor = gain[:, lanes]

        @pl.loop(0, KEY_TILES // 2)
        def _(n):
            at = pl.ds(pl.multiple_of(n * 2 * T, 2 * T), 2 * T)
            scaled[at, :] = (raw[at, :].astype(F32) * factor).astype(BF16)

    for copy in loads[2:]:
        copy.wait()
    run(0, whole, False, 2, 8)
    run(base_both, both, True, 2, 4)
    run(base_one, one, True, 1, 4)

    @pl.loop(0, QUERY_TILES)
    def _(i):
        rows = pl.ds(pl.multiple_of(i * T, T), T)
        for h in range(HEADS):
            lanes = slice(h * D, (h + 1) * D)
            dq_ref[rows, lanes] = (dq_acc[i, :, lanes] * scale).astype(BF16).T

    gain_acc[...] = jnp.zeros_like(gain_acc)

    @pl.loop(0, KEY_TILES)
    def _(n):
        at = pl.ds(pl.multiple_of(n * T, T), T)
        dkey, dvalue = dk_acc[at, :] * scale, dv_acc[at, :]
        owner = (lax.div(n, 16), lax.rem(lax.div(n, 4), 4), lax.rem(n, 4))
        dk_ref[owner] = dkey.astype(BF16)
        dv_ref[owner] = dvalue.astype(BF16)
        gain_acc[0] += jnp.sum((dkey * keys[at, :].astype(F32)).reshape(T // 8, 8, D), axis=0)
        gain_acc[1] += jnp.sum((dvalue * values[at, :].astype(F32)).reshape(T // 8, 8, D), axis=0)

    gains[...] = jnp.zeros_like(gains)
    for n in range(2):
        gains[n : n + 1, :] = jnp.sum(gain_acc[n], axis=0, keepdims=True)


def scatter(
    dq, dk, dv, partial, key_gain, value_gain,
    grad_queries, grad_keys, grad_values, grad_key_gain, grad_value_gain,
    dq_in, land_z, land_v, land_k, out_k, out_v, in_k, in_v, near, total, sends, recvs,
):
    z, y, x, c = place()
    ka = lax.rem(z, 2) * 4 + x
    z_hi, z_lo = lax.div(z, 2), lax.rem(z, 2)
    y_plus, y_minus = ident(z, wrap(y + 1), x, c), ident(z, wrap(y - 1), x, c)
    z_far, z_near = ident(wrap(z + 2 * z_lo - 1), y, x, c), ident(wrap(z + 1 - 2 * z_lo), y, x, c)
    steps = [(one, two) for one in range(RING) for two in range(RING) if one or two]
    in_y = [ident(z, wrap(y + one), wrap(x + two), c) for one, two in steps]
    in_z = [ident(wrap(z + one), y, wrap(x + two), c) for one, two in steps]
    others = [(0, one, ident(wrap(z + one), y, x, c)) for one in range(1, RING)]
    others += [(1, one, ident(wrap(z + one), y, x, 1 - c)) for one in range(RING)]
    greet(in_y + [peer for peer, (one, _) in zip(in_z, steps) if one] + [other for flip, _, other in others if flip])

    spread = Lane(sends, recvs, 56)
    for (one, two), peer in zip(steps, in_y):
        spread.send(partial, near.at[one, two], one * RING + two, peer)
    near[0, 0] = partial[...]

    sibling = ident(z, y, x, 1 - c)
    pair = Lane(sends, recvs, 0)
    for n in range(KA):
        to = lax.rem(ka + n + 1, KA)
        rows = pl.ds(pl.multiple_of(((1 - c) * KA + to) * T, T), T)
        pair.send(dq.at[rows], dq_in.at[to], n, sibling)

    keys_z = Detour(sends, recvs, 16).setup(
        lambda at: dk.at[at, :, pl.ds(0, Z_FIRST)], [pl.ds(0, 2), pl.ds(2, 2)], land_z, z, z_far, z_near
    )
    last_y = Fold(sends, recvs, 22).setup(
        lambda off, n: dk.at[pl.ds(2 * n, 2), wrap(y + off), pl.ds(Z_FIRST, RING - Z_FIRST)], land_k, y_plus, y_minus
    )
    rows_of = [pl.ds(n * (T // PARTS), T // PARTS) for n in range(PARTS)]
    values_y = [
        Fold(sends, recvs, 72 + 22 * part).setup(
            lambda off, n, rows=rows: dv.at[pl.ds(2 * n, 2), wrap(y + off), :, rows], land_v.at[part], y_plus, y_minus
        )
        for part, rows in enumerate(rows_of)
    ]
    keys_z.start()
    last_y.start()
    for lane in values_y:
        lane.start()

    lane_q = Lane(sends, recvs, 8)
    columns = head_columns(z, x)
    for n in range(KA):
        to = lax.rem(ka + n + 1, KA)
        own_rows = dq.at[pl.ds(pl.multiple_of((c * KA + to) * T, T), T)]
        pair.arrive(dq_in.at[to], n, sibling)
        for h in range(HEADS):
            lanes = pl.ds(h * D, D)
            value = own_rows[:, lanes].astype(F32) + dq_in[to, :, lanes].astype(F32)
            dq_in[to, :, lanes] = value.astype(BF16)
        if n < KA - 1:
            peer = ident(z_hi * 2 + lax.div(to, 4), y, lax.rem(to, 4), c)
            lane_q.send(dq_in.at[to], grad_queries.at[:, columns], n + 1, peer)
    grad_queries[:, columns] = dq_in[ka]

    for (one, two), peer in zip(steps, in_y):
        spread.arrive(near.at[one, two], one * RING + two, peer)
    for n in range(RING):
        block = near[wrap(y), wrap(x - n + RING)]
        for one in range(1, RING):
            block = block + near[wrap(y - one + RING), wrap(x - n + RING)]
        total[0, 2 * n : 2 * n + 2, :] = block[0:2]
    mine = c * RING + z
    total[1 + mine] = total[0]
    share = Lane(sends, recvs, 28)
    for flip, step, other in others:
        share.send(total.at[0], total.at[1 + mine], flip * RING + step, other)

    def finish_values(part):
        values_y[part].finish([out_v.at[pl.ds(2 * n, 2), :, rows_of[part]] for n in range(2)])

    last_y.relay()
    keys_z.relay(0)
    values_y[0].relay()
    keys_z.relay(1)
    last_y.finish([out_k.at[pl.ds(2 * n, 2), pl.ds(Z_FIRST, RING - Z_FIRST)] for n in range(2)])
    finish_values(0)

    def send_values(part):
        lane = Lane(sends, recvs, 78 + 22 * part)
        for (one, two), peer in zip(steps, in_z):
            block = out_v.at[wrap(z + one), wrap(x + two), rows_of[part]]
            lane.send(block, in_v.at[one, two, rows_of[part]], one * RING + two, peer)
        return lane

    values_out = [send_values(0)]
    for part in range(1, PARTS):
        values_y[part].relay()
        finish_values(part)
        values_out.append(send_values(part))
    keys_z.finish(out_k.at[:, pl.ds(0, Z_FIRST)])
    keys_out = Lane(sends, recvs, 40)
    for one, two in steps:
        to = wrap(x + two)
        over_z = lax.div(to, Z_FIRST)
        to_z, to_y = wrap(z + one * over_z), wrap(y + one * (1 - over_z))
        block = out_k.at[over_z * to_z + (1 - over_z) * to_y, to]
        keys_out.send(block, in_k.at[one, two], one * RING + two, ident(to_z, to_y, to, c))

    def deliver(result, gain, own, came):
        for two in range(RING):
            lanes = pl.ds(pl.multiple_of(wrap(x - two) * D, D), D)
            value = (own if two == 0 else came[0, two]).astype(F32)
            for one in range(1, RING):
                value = value + came[one, two].astype(F32)
            result[:, lanes] = (value * gain[:, lanes]).astype(BF16)

    for (one, two), peer in zip(steps, in_y):
        keys_out.arrive(in_k.at[one, two], one * RING + two, peer)
    own_over_z = lax.div(x, Z_FIRST)
    deliver(grad_keys, key_gain, out_k[own_over_z * z + (1 - own_over_z) * y, x], in_k)
    for part in range(PARTS):
        for (one, two), peer in zip(steps, in_z):
            values_out[part].arrive(in_v.at[one, two, rows_of[part]], one * RING + two, peer)
    deliver(grad_values, value_gain, out_v[z, x], in_v)

    for flip, step, other in others:
        origin = (1 - c if flip else c) * RING + wrap(z - step)
        share.arrive(total.at[1 + origin], flip * RING + step, other)
    whole = jnp.sum(total[1:], axis=0)
    for n in range(RING):
        grad_key_gain[:, n * D : (n + 1) * D] = whole[2 * n : 2 * n + 1]
        grad_value_gain[:, n * D : (n + 1) * D] = whole[2 * n + 1 : 2 * n + 2]
    for n in range(1, KA):
        origin = lax.rem(ka + KA - n, KA)
        their = head_columns(lax.div(origin, 4), lax.rem(origin, 4))
        from_ = ident(z_hi * 2 + lax.div(origin, 4), y, lax.rem(origin, 4), c)
        lane_q.arrive(grad_queries.at[:, their], n, from_)
    for lane in [
        pair, lane_q, keys_z, last_y, *values_y, keys_out, *values_out, share, spread
    ]:
        lane.drain()


def shape(dims, dtype):
    return jax.ShapeDtypeStruct(dims, dtype)


def attend_call(table, stats, queries, grad_out, sibling_rows, k, v, key_gain, value_gain):
    vm, hbm = pl.BlockSpec(memory_space=pltpu.VMEM), pl.BlockSpec(memory_space=pl.ANY)
    return pl.pallas_call(
        attend,
        out_shape=(shape((2 * KA * T, WIDTH), BF16), *[shape((RING, RING, RING, T, D), BF16)] * 2, shape((8, D), F32)),
        in_specs=[pl.BlockSpec(memory_space=pltpu.SMEM)] + [hbm] * 6 + [vm] * 2,
        out_specs=(vm,) * 4,
        scratch_shapes=[
            pltpu.SMEM((QUERY_TILES * KEY_TILES // 2 + 2 * QUERY_TILES + 4,), jnp.int32),
            pltpu.VMEM(stats.shape, F32),
            pltpu.VMEM((2 * KA * T, WIDTH), BF16),
            pltpu.VMEM((2 * KA * T, WIDTH), BF16),
            pltpu.VMEM(k.shape, BF16),
            pltpu.VMEM(v.shape, BF16),
            pltpu.VMEM(k.shape, BF16),
            pltpu.VMEM(v.shape, BF16),
            pltpu.VMEM(k.shape, F32),
            pltpu.VMEM(v.shape, F32),
            pltpu.VMEM((QUERY_TILES, D, WIDTH), F32),
            pltpu.VMEM((2, 2, 2 * T, WIDTH), BF16),
            pltpu.VMEM((2, 8, D), F32),
            pltpu.SemaphoreType.DMA((7,)),
        ],
        compiler_params=pltpu.CompilerParams(vmem_limit_bytes=47 * 2**20),
        name="attend",
    )(table, stats, queries, grad_out, sibling_rows, k, v, key_gain, value_gain)


def shards(
    queries, key_rows, values, attn_out, grad_out, log_sums, key_gain, value_gain, doc_ids, tile_mask, block_order
):
    vm, hbm = pl.BlockSpec(memory_space=pltpu.VMEM), pl.BlockSpec(memory_space=pl.ANY)
    key_gain, value_gain = key_gain.reshape(1, -1), value_gain.reshape(1, -1)
    rows = queries.shape[0]
    sibling_rows, kg, vg, stats, table = pl.pallas_call(
        gather,
        out_shape=(
            shape((2, rows, WIDTH), BF16),
            shape((RING, RING, RING * T, D), BF16),
            shape((RING, RING, RING * T, D), BF16),
            shape((QUERY_TILES, 2 * HEADS, T), F32),
            shape((QUERY_TILES, T), jnp.int32),
        ),
        in_specs=[hbm] * 9,
        out_specs=(hbm,) * 5,
        scratch_shapes=[
            pltpu.VMEM((QUERY_TILES, T), jnp.int32),
            pltpu.VMEM(attn_out.shape, BF16),
            pltpu.VMEM(log_sums.shape, F32),
            pltpu.VMEM((1, T), jnp.int32),
            pltpu.VMEM(tile_mask.shape, jnp.int32),
            pltpu.VMEM((1, T), jnp.int32),
            pltpu.VMEM(attn_out.shape, BF16),
            pltpu.VMEM((KA, 2 * HEADS, T), F32),
            pltpu.SemaphoreType.DMA((64,)),
            pltpu.SemaphoreType.DMA((64,)),
            pltpu.SemaphoreType.DMA((12,)),
        ],
        compiler_params=pltpu.CompilerParams(
            collective_id=0, has_side_effects=True, vmem_limit_bytes=56 * 2**20
        ),
        name="gather",
    )(
        queries, grad_out, key_rows, values, attn_out, log_sums,
        doc_ids.reshape(1, -1), tile_mask, block_order.reshape(1, -1),
    )
    dq, dk, dv, partial = attend_call(
        table, stats, queries, grad_out, sibling_rows,
        kg.reshape(KEY_TILES * T, D), vg.reshape(KEY_TILES * T, D), key_gain, value_gain,
    )
    grad_queries, grad_keys, grad_values, grad_key_gain, grad_value_gain = pl.pallas_call(
        scatter,
        out_shape=(
            shape(attn_out.shape, BF16),
            shape(key_rows.shape, BF16),
            shape(values.shape, BF16),
            shape(key_gain.shape, F32),
            shape(value_gain.shape, F32),
        ),
        in_specs=[vm] * 6,
        out_specs=(vm,) * 5,
        scratch_shapes=[
            pltpu.VMEM((KA, T, WIDTH), BF16),
            pltpu.VMEM((3, RING, Z_FIRST, T, D), BF16),
            pltpu.VMEM((PARTS, 6, 2, RING, T // PARTS, D), BF16),
            pltpu.VMEM((6, 2, RING - Z_FIRST, T, D), BF16),
            pltpu.VMEM((RING, RING, T, D), BF16),
            pltpu.VMEM((RING, RING, T, D), BF16),
            pltpu.VMEM((RING, RING, T, D), BF16),
            pltpu.VMEM((RING, RING, T, D), BF16),
            pltpu.VMEM((RING, RING, 8, D), F32),
            pltpu.VMEM((9, 8, D), F32),
            pltpu.SemaphoreType.DMA((72 + 22 * PARTS,)),
            pltpu.SemaphoreType.DMA((72 + 22 * PARTS,)),
        ],
        compiler_params=pltpu.CompilerParams(
            collective_id=1, has_side_effects=True, vmem_limit_bytes=20 * 2**20
        ),
        name="scatter",
    )(dq, dk, dv, partial, key_gain, value_gain)
    return grad_queries, grad_keys, grad_values, grad_key_gain.reshape(-1), grad_value_gain.reshape(-1)


def solution(mesh):
    rows = P(("pb", "ka"), None)
    placed = (P("pb", None), rows, rows, rows, P("pb", None), P(None, ("pb", "ka")), P(), P(), P(), P(), P())
    return jax.shard_map(
        shards, mesh=mesh, in_specs=placed, out_specs=(rows, rows, rows, P(), P()), check_vma=False
    )
```
